32 devices in a mesh: groups: 2 (over y), ctx: 8 (over z, x), ch: 2 (over core).
Axes of the slice: x: 2, y: 2, z: 4, core: 2. Of those that a mesh axis runs over, the one named last changes fastest.
Arguments:
- gate_stream: bfloat16 [4096, 512], P(('groups', 'ctx'), 'ch'), parts along dimension 0, may hold values from -6 to 6
- outer_stream: bfloat16 [4096, 512], P(('groups', 'ctx'), 'ch'), parts along dimension 0, may hold values from -6 to 6
- value_stream: bfloat16 [4096, 512], P(('groups', 'ctx'), 'ch'), parts along dimension 0, may hold values from -6 to 6
- short_weight: bfloat16 [3, 3, 512], P(None, None, 'ch'), may hold values from -3.5 to 3.5
- long_filter: bfloat16 [2048, 512], P('ctx', 'ch'), may hold values from -0.125 to 0.125
- skip_gain: float32 [512], P('ch'), may hold values from -4 to 4
Outputs:
- output_rows: bfloat16 [4096, 512], P(('groups', 'ctx'), 'ch'), parts along dimension 0
The draws below stay inside these ranges and needn't reach their ends.
There are 2 independent parts, one for each index of `groups`. The reference program is written for one: setup_inputs(seed, part) draws one part's arguments, and reference() takes and returns one part's arrays. A program takes and returns all parts, laid end to end along the dimension named above; an argument that names none is the same for every part. Nothing has to cross between parts.
All inputs are finite; a program needn't handle non-finite values.
Results may differ from the reference program's by a relative error of at most 0.001.
Values may be sent and summed in bfloat16 or wider, within the bound.
A program may use at most 64 MiB of HBM per device.

```python
import jax
import jax.numpy as jnp

CH = 512
TAPS = 3
SEQ = 2048


def block_levels(key, dims, cuts, smallest, top_value):
    def one(dim, shards_of):
        draws = jax.random.uniform(jax.random.fold_in(jax.random.fold_in(key, 6), dim), (shards_of,), jnp.float32, smallest / len(cuts), top_value / len(cuts))
        return jnp.repeat(jnp.exp(draws), dims[dim] // shards_of).reshape((-1,) + (1,) * (len(dims) - dim - 1))

    gain = one(*cuts[0])
    for cut in cuts[1:]:
        gain = gain * one(*cut)
    return gain


def normal_values(stream_key, shape, width, bound, shards=(), kind=jnp.bfloat16):
    result = jax.random.normal(stream_key, shape, jnp.float32) * width
    if len(shards) > 0:
        result = block_levels(stream_key, shape, shards, -0.22, 0.18) * result
    return jnp.clip(result, min=-bound, max=bound).astype(kind)


def setup_inputs(seed: int = 0, part: int = 0) -> dict:
    arg_keys = jax.random.split(jax.random.key(seed), 7)
    part_splits = jax.random.split(jax.random.fold_in(arg_keys[6], part), 7)
    gate_stream = normal_values(part_splits[0], (SEQ, CH), 1.0, 6.0, ((0, 8), (1, 2)))
    outer_stream = normal_values(part_splits[1], (SEQ, CH), 1.0, 6.0, ((0, 8), (1, 2)))
    value_stream = normal_values(part_splits[2], (SEQ, CH), 1.0, 6.0, ((0, 8), (1, 2)))
    short_weight = normal_values(arg_keys[3], (3, TAPS, CH), TAPS ** -0.5, 3.5, ((2, 2),))
    long_filter = normal_values(arg_keys[4], (SEQ, CH), SEQ ** -0.5, 0.125, ((0, 8), (1, 2)))
    skip_gain = normal_values(arg_keys[5], (CH,), 1.0, 4.0, ((0, 2),), jnp.float32)
    return {"gate_stream": gate_stream, "outer_stream": outer_stream, "value_stream": value_stream, "short_weight": short_weight, "long_filter": long_filter, "skip_gain": skip_gain}


def short_conv(stream, kernel):
    padded = jnp.pad(stream.astype(jnp.float32), ((TAPS - 1, 0), (0, 0)))
    summed = jnp.zeros(stream.shape, jnp.float32)
    for offset in range(TAPS):
        begin_at = TAPS - 1 - offset
        summed = summed + kernel[offset].astype(jnp.float32) * padded[begin_at:begin_at + SEQ]
    return summed


def reference(gate_stream, outer_stream, value_stream, short_weight, long_filter, skip_gain):
    gate_conv = short_conv(gate_stream, short_weight[0])
    outer_conv = short_conv(outer_stream, short_weight[1])
    value_conv = short_conv(value_stream, short_weight[2])
    gated_value = gate_conv * value_conv
    spectrum = jnp.fft.rfft(gated_value, n=2 * SEQ, axis=0) * jnp.fft.rfft(long_filter.astype(jnp.float32), n=2 * SEQ, axis=0)
    long_part = jnp.fft.irfft(spectrum, n=2 * SEQ, axis=0)[:SEQ]
    output_rows = outer_conv * (long_part + skip_gain[None, :] * gated_value)
    return output_rows.astype(jnp.bfloat16)
```

```python
import functools

import jax
import jax.numpy as jnp
import numpy as np
from jax import lax
from jax.experimental import pallas as pl
from jax.experimental.pallas import tpu as pltpu
from jax.sharding import PartitionSpec as P

LANES = 128
RIM = 8


def loop(begin, end, step, carry):
    if end - begin <= 8:
        for i in range(begin, end):
            carry = step(i, carry)
        return carry
    return lax.fori_loop(begin, end, step, carry)


def transform_table(rows):
    freq = np.arange(rows)[:, None]
    time = np.arange(rows)[None, :]
    phase = ((2 * freq + 1) * time % (4 * rows)) * (np.pi / (2 * rows))
    return np.concatenate([np.cos(phase), -np.sin(phase)], axis=0)


def split(table):
    table = np.asarray(table, np.float32)
    high = table.astype(jnp.bfloat16)
    low = (table - high.astype(np.float32)).astype(jnp.bfloat16)
    return np.stack([high, low])


def halves(value):
    high = value.astype(jnp.bfloat16)
    low = (value - high.astype(jnp.float32)).astype(jnp.bfloat16)
    return high, low


def dot(a, b):
    return jnp.dot(a, b, preferred_element_type=jnp.float32)


def lane_group(rows, width):
    return lax.broadcasted_iota(jnp.int32, (rows, LANES), 1) // width


def exchange_groups(parts, width):
    parts = list(parts)
    count = LANES // width
    group = lane_group(parts[0].shape[0], width)
    span = 1
    while span < count:
        keep = (group & span) == 0
        for q in range(count):
            if q & span == 0:
                low, high = parts[q], parts[q | span]
                parts[q] = jnp.where(keep, low, pltpu.roll(high, span * width, 1))
                parts[q | span] = jnp.where(keep, pltpu.roll(low, LANES - span * width, 1), high)
        span *= 2
    return parts


def kernel(
    devices, gate, outer, value, weight, filt, skip, table, back_table, out,
    ext, tail, rim, send_h, recv_h, send_g, recv_g, send_r, recv_r, spec, spread, prod, kept,
    rim_send, rim_recv, h_send, h_recv, g_send, g_recv, r_send, r_recv,
):
    rows, channels = gate.shape
    width = channels // devices
    count = LANES // width
    piece = rows // count
    tiles = channels // LANES
    me = lax.axis_index("ctx")

    def partner(distance):
        return lax.rem(me + distance, devices)

    barrier = pltpu.get_barrier_semaphore()

    def greet(distance, carry):
        pl.semaphore_signal(
            barrier, inc=1, device_id={"ctx": partner(distance)}, device_id_type=pl.DeviceIdType.MESH
        )
        return carry

    loop(1, devices, greet, 0)

    for i, stream in enumerate((gate, outer, value)):
        ext[i, RIM:, :] = stream[...].astype(jnp.float32)
        tail[i] = ext[i, rows:, :]

    def pack(source, send, recv):
        for tile in range(tiles):
            parts = [
                source(q * piece, tile * LANES).astype(jnp.float32) for q in range(count)
            ]
            for q, part in enumerate(exchange_groups(parts, width)):
                send[tile * count + q] = part.astype(send.dtype)
        recv[pl.ds(me, 1)] = send[pl.ds(me, 1)]

    def unpack(recv, tile):
        parts = [recv[tile * count + q].astype(jnp.float32) for q in range(count)]
        return jnp.concatenate(exchange_groups(parts, width), axis=0)

    def exchange(send, recv, send_sem, recv_sem, act):
        def step(distance, carry):
            copy = pltpu.make_async_remote_copy(
                src_ref=send.at[partner(distance)],
                dst_ref=recv.at[me],
                send_sem=send_sem.at[distance],
                recv_sem=recv_sem.at[distance],
                device_id={"ctx": partner(distance)},
                device_id_type=pl.DeviceIdType.MESH,
            )
            act(copy)
            return carry

        loop(1, devices, step, 0)

    pl.semaphore_wait(barrier, devices - 1)
    rim_copy = pltpu.make_async_remote_copy(
        src_ref=tail,
        dst_ref=rim,
        send_sem=rim_send,
        recv_sem=rim_recv,
        device_id={"ctx": partner(1)},
        device_id_type=pl.DeviceIdType.MESH,
    )
    rim_copy.start()

    pack(lambda r, c: filt[r : r + piece, c : c + LANES], send_h, recv_h)
    exchange(send_h, recv_h, h_send, h_recv, lambda copy: copy.start())

    rim_copy.wait()
    for i in range(3):
        ext[i, :RIM, :] = jnp.where(me > 0, rim[i], 0.0)

    def short(i, r, c):
        taps = weight[i].astype(jnp.float32)
        total = None
        for offset in range(taps.shape[0]):
            term = taps[offset : offset + 1, c : c + LANES] * ext[
                i, r + RIM - offset : r + RIM - offset + piece, c : c + LANES
            ]
            total = term if total is None else total + term
        return total

    def gated(r, c):
        result = short(0, r, c) * short(2, r, c)
        kept[r : r + piece, c : c + LANES] = result
        return result

    pack(gated, send_g, recv_g)
    exchange(send_g, recv_g, g_send, g_recv, lambda copy: copy.start())

    exchange(send_h, recv_h, h_send, h_recv, lambda copy: copy.wait_recv())
    for tile in range(tiles):
        taps = unpack(recv_h, tile).astype(jnp.bfloat16)
        spec[:, tile * LANES : (tile + 1) * LANES] = dot(table[0], taps) + dot(table[1], taps)
    chunk = 16
    group = lane_group(chunk, width)
    sign = 1.0 - 2.0 * (lax.broadcasted_iota(jnp.int32, (chunk, LANES), 0) % 2).astype(jnp.float32)

    def load(ref, start, tile):
        lanes = slice(tile * LANES, (tile + 1) * LANES)
        return (
            ref[pl.ds(pl.multiple_of(start, chunk), chunk), lanes],
            ref[pl.ds(pl.multiple_of(rows + start, chunk), chunk), lanes],
        )

    def shifted(blocks, tile, places):
        turned = pltpu.roll(blocks[tile], places * width, 1)
        before = pltpu.roll(blocks[tile - 1], places * width, 1) if tile > 0 else 0.0
        return jnp.where(group >= places, turned, before)

    def spread_chunk(index, carry):
        start = index * chunk
        at = pl.ds(pl.multiple_of(start, chunk), chunk)
        loaded = [load(spec, start, tile) for tile in range(tiles)]
        real = [pair[0] for pair in loaded]
        imag = [pair[1] for pair in loaded]
        for tile in range(tiles):
            both = (
                real[tile] - sign * shifted(imag, tile, 1),
                imag[tile] + sign * shifted(real, tile, 1),
            )
            for part, block in enumerate(both):

                def place(k, carry):
                    only = jnp.where(group == k, block, 0.0)
                    only = pltpu.roll(only, lax.rem(LANES - k * width, LANES), 1)
                    span = 1
                    while span < count:
                        only = only + pltpu.roll(only, span * width, 1)
                        span *= 2
                    spread[k, tile, part, at, :] = only
                    return carry

                loop(0, count, place, 0)
        return carry

    lax.fori_loop(0, rows // chunk, spread_chunk, 0)

    exchange(send_g, recv_g, g_send, g_recv, lambda copy: copy.wait_recv())
    for tile in range(tiles):
        high, low = halves(unpack(recv_g, tile))
        spec[:, tile * LANES : (tile + 1) * LANES] = (
            dot(table[0], high) + dot(table[1], high) + dot(table[0], low)
        )

    def product_chunk(index, carry):
        start = index * chunk
        at = pl.ds(pl.multiple_of(start, chunk), chunk)
        also = pl.ds(pl.multiple_of(rows + start, chunk), chunk)
        loaded = [load(spec, start, tile) for tile in range(tiles)]
        real = [pair[0] for pair in loaded]
        imag = [pair[1] for pair in loaded]

        def step(k, sums):
            sums = list(sums)
            moved_real = [shifted(real, tile, k) for tile in range(tiles)]
            moved_imag = [shifted(imag, tile, k) for tile in range(tiles)]
            for apart in range(tiles):
                kr = spread[k, apart, 0, at, :]
                ki = spread[k, apart, 1, at, :]
                for tile in range(apart, tiles):
                    xr, xi = moved_real[tile - apart], moved_imag[tile - apart]
                    sums[2 * tile] = sums[2 * tile] + (xr * kr - xi * ki)
                    sums[2 * tile + 1] = sums[2 * tile + 1] + (xr * ki + xi * kr)
            return tuple(sums)

        sums = loop(0, count, step, (jnp.zeros((chunk, LANES), jnp.float32),) * (2 * tiles))
        for tile in range(tiles):
            lanes = slice(tile * LANES, (tile + 1) * LANES)
            for where, total in ((at, sums[2 * tile]), (also, sums[2 * tile + 1])):
                high, low = halves(total)
                prod[0, where, lanes] = high
                prod[1, where, lanes] = low
        return carry

    lax.fori_loop(0, rows // chunk, product_chunk, 0)

    for tile in range(tiles):
        lanes = slice(tile * LANES, (tile + 1) * LANES)
        high, low = prod[0, :, lanes], prod[1, :, lanes]
        long_rows = dot(back_table[0], high) + dot(back_table[1], high) + dot(back_table[0], low)
        parts = [long_rows[q * piece : (q + 1) * piece] for q in range(count)]
        for q, part in enumerate(exchange_groups(parts, width)):
            send_r[tile * count + q] = part
    recv_r[pl.ds(me, 1)] = send_r[pl.ds(me, 1)]
    exchange(send_r, recv_r, r_send, r_recv, lambda copy: copy.start())

    for tile in range(tiles):
        for q in range(count):
            r, c = q * piece, tile * LANES
            ext[0, r : r + piece, c : c + LANES] = short(1, r, c)
    exchange(send_h, recv_h, h_send, h_recv, lambda copy: copy.wait_send())
    exchange(send_g, recv_g, g_send, g_recv, lambda copy: copy.wait_send())
    exchange(send_r, recv_r, r_send, r_recv, lambda copy: copy.wait_recv())
    for tile in range(tiles):
        lanes = slice(tile * LANES, (tile + 1) * LANES)
        long_part = unpack(recv_r, tile)
        out[:, lanes] = (
            ext[0, :rows, lanes] * (long_part + skip[:, lanes] * kept[:, lanes])
        ).astype(out.dtype)
    exchange(send_r, recv_r, r_send, r_recv, lambda copy: copy.wait_send())


def body(gate_stream, outer_stream, value_stream, short_weight, long_filter, skip_gain):
    devices = lax.axis_size("ctx")
    rows, channels = gate_stream.shape
    width = channels // devices
    count = LANES // width
    piece = rows // count
    tiles = channels // LANES
    table = transform_table(rows)
    filter_type = jnp.bfloat16 if piece % 16 == 0 else jnp.float32
    full = pltpu.VMEM((devices, piece, LANES), jnp.float32)
    part = pltpu.VMEM((devices, piece, LANES), filter_type)
    many = pltpu.SemaphoreType.DMA((devices,))
    vmem = pl.BlockSpec(memory_space=pltpu.VMEM)
    return pl.pallas_call(
        functools.partial(kernel, devices),
        out_shape=jax.ShapeDtypeStruct((rows, channels), jnp.bfloat16),
        in_specs=[vmem] * 8,
        out_specs=vmem,
        scratch_shapes=[
            pltpu.VMEM((3, RIM + rows, channels), jnp.float32),
            pltpu.VMEM((3, RIM, channels), jnp.float32),
            pltpu.VMEM((3, RIM, channels), jnp.float32),
            part, part, full, full, full, full,
            pltpu.VMEM((2 * rows, channels), jnp.float32),
            pltpu.VMEM((count, tiles, 2, rows, LANES), jnp.float32),
            pltpu.VMEM((2, 2 * rows, channels), jnp.bfloat16),
            pltpu.VMEM((rows, channels), jnp.float32),
            pltpu.SemaphoreType.DMA,
            pltpu.SemaphoreType.DMA,
            many, many, many, many, many, many,
        ],
        compiler_params=pltpu.CompilerParams(
            collective_id=0, has_side_effects=True, vmem_limit_bytes=48 * 1024 * 1024
        ),
        cost_estimate=pl.CostEstimate(
            flops=2 * 16 * rows * rows * channels, bytes_accessed=4 * rows * channels, transcendentals=0
        ),
    )(
        gate_stream, outer_stream, value_stream, short_weight, long_filter, skip_gain[None, :],
        jnp.asarray(split(table)), jnp.asarray(split(table.T / rows)),
    )


def solution(mesh):
    placed = (
        P(("groups", "ctx"), "ch"),
        P(("groups", "ctx"), "ch"),
        P(("groups", "ctx"), "ch"),
        P(None, None, "ch"),
        P("ctx", "ch"),
        P("ch"),
    )
    return jax.shard_map(
        body, mesh=mesh, in_specs=placed, out_specs=P(("groups", "ctx"), "ch"), check_vma=False
    )
```

```python
import functools

import jax
import jax.numpy as jnp
import numpy as np
from jax import lax
from jax.experimental import pallas as pl
from jax.experimental.pallas import tpu as pltpu
from jax.sharding import PartitionSpec as P

LANES = 128
RIM = 8


def loop(begin, end, step, carry):
    if end - begin <= 8:
        for i in range(begin, end):
            carry = step(i, carry)
        return carry
    return lax.fori_loop(begin, end, step, carry)


def transform_table(rows):
    freq = np.arange(rows)[:, None]
    time = np.arange(rows)[None, :]
    phase = ((2 * freq + 1) * time % (4 * rows)) * (np.pi / (2 * rows))
    return np.concatenate([np.cos(phase), -np.sin(phase)], axis=0)


def split(table):
    table = np.asarray(table, np.float32)
    high = table.astype(jnp.bfloat16)
    low = (table - high.astype(np.float32)).astype(jnp.bfloat16)
    return np.stack([high, low])


def halves(value):
    high = value.astype(jnp.bfloat16)
    low = (value - high.astype(jnp.float32)).astype(jnp.bfloat16)
    return high, low


def dot(a, b):
    return jnp.dot(a, b, preferred_element_type=jnp.float32)


def lane_group(rows, width):
    return lax.broadcasted_iota(jnp.int32, (rows, LANES), 1) // width


def exchange_groups(parts, width):
    parts = list(parts)
    count = LANES // width
    group = lane_group(parts[0].shape[0], width)
    span = 1
    while span < count:
        keep = (group & span) == 0
        for q in range(count):
            if q & span == 0:
                low, high = parts[q], parts[q | span]
                parts[q] = jnp.where(keep, low, pltpu.roll(high, span * width, 1))
                parts[q | span] = jnp.where(keep, pltpu.roll(low, LANES - span * width, 1), high)
        span *= 2
    return parts


def spread_groups(block, width):
    count = LANES // width
    group = lane_group(block.shape[0], width)
    result = [block]
    span = count // 2
    while span:
        keep = (group & span) == 0
        wider = []
        for each in result:
            turned = pltpu.roll(each, span * width, 1)
            wider += [jnp.where(keep, each, turned), jnp.where(keep, turned, each)]
        result = wider
        span //= 2
    return result


def kernel(
    devices, shares, gate_hbm, outer_hbm, value_hbm, weight_hbm, filt_hbm, skip_hbm,
    table_hbm, back_hbm, out,
    gate, outer, value, weight, filt, skip, table, back_table,
    ext, tail, rim, send_h, recv_h, send_g, recv_g, send_r, recv_r, spec, spread, prod, kept,
    load_sem, rim_send, rim_recv, h_send, h_recv, g_send, g_recv, r_send, r_recv,
):
    rows, channels = gate.shape
    width = channels // (devices * shares)
    count = LANES // width
    piece = rows // count
    tiles = channels // LANES
    share_tiles = tiles // shares
    me = lax.axis_index("ctx")

    def partner(distance):
        return lax.rem(me + distance, devices)

    barrier = pltpu.get_barrier_semaphore()

    def greet(distance, carry):
        pl.semaphore_signal(
            barrier, inc=1, device_id={"ctx": partner(distance)}, device_id_type=pl.DeviceIdType.MESH
        )
        return carry

    loop(1, devices, greet, 0)

    pairs = (
        (gate_hbm, gate), (value_hbm, value), (filt_hbm, filt), (weight_hbm, weight),
        (outer_hbm, outer), (skip_hbm, skip), (table_hbm, table), (back_hbm, back_table),
    )
    loads = [pltpu.make_async_copy(src, dst, load_sem.at[i]) for i, (src, dst) in enumerate(pairs)]
    for load in loads:
        load.start()

    def place_of(tile, q):
        return divmod(tile * count + q, shares)

    def pack(source, send):
        for tile in range(tiles):
            parts = [
                source(q * piece, tile * LANES).astype(jnp.float32) for q in range(count)
            ]
            for q, part in enumerate(exchange_groups(parts, width)):
                device, share = place_of(tile, q)
                send[share, device] = part.astype(send.dtype)

    def unpack(recv, share, tile):
        parts = [recv[share, tile * count + q].astype(jnp.float32) for q in range(count)]
        return jnp.concatenate(exchange_groups(parts, width), axis=0)

    def exchange(send, recv, send_sem, recv_sem, share, act):
        def step(distance, carry):
            copy = pltpu.make_async_remote_copy(
                src_ref=send.at[share, partner(distance)],
                dst_ref=recv.at[share, me],
                send_sem=send_sem.at[share, distance],
                recv_sem=recv_sem.at[share, distance],
                device_id={"ctx": partner(distance)},
                device_id_type=pl.DeviceIdType.MESH,
            )
            act(copy)
            return carry

        loop(1, devices, step, 0)

    def keep_own(send, recv, share):
        recv[share, pl.ds(me, 1)] = send[share, pl.ds(me, 1)]

    def start(copy):
        copy.start()

    def arrived(copy):
        copy.wait_recv()

    def left(copy):
        copy.wait_send()

    loads[0].wait()
    loads[1].wait()
    loads[4].wait()
    for i, stream in enumerate((gate, outer, value)):
        ext[i, RIM:, :] = stream[...].astype(jnp.float32)
        tail[i] = ext[i, rows:, :]
    loads[2].wait()
    pack(lambda r, c: filt[r : r + piece, c : c + LANES], send_h)

    pl.semaphore_wait(barrier, devices - 1)
    rim_copy = pltpu.make_async_remote_copy(
        src_ref=tail,
        dst_ref=rim,
        send_sem=rim_send,
        recv_sem=rim_recv,
        device_id={"ctx": partner(1)},
        device_id_type=pl.DeviceIdType.MESH,
    )
    rim_copy.start()
    for share in range(shares):
        exchange(send_h, recv_h, h_send, h_recv, share, start)
        keep_own(send_h, recv_h, share)
    loads[3].wait()

    rim_copy.wait()
    for i in range(3):
        ext[i, :RIM, :] = jnp.where(me > 0, rim[i], 0.0)

    def short(i, r, c):
        taps = weight[i].astype(jnp.float32)
        total = None
        for offset in range(taps.shape[0]):
            term = taps[offset : offset + 1, c : c + LANES] * ext[
                i, r + RIM - offset : r + RIM - offset + piece, c : c + LANES
            ]
            total = term if total is None else total + term
        return total

    def gated(r, c):
        result = short(0, r, c) * short(2, r, c)
        kept[r : r + piece, c : c + LANES] = result
        return result

    pack(gated, send_g)
    for share in range(shares):
        exchange(send_g, recv_g, g_send, g_recv, share, start)
    for share in range(shares):
        keep_own(send_g, recv_g, share)
    for load in loads[5:]:
        load.wait()

    chunk = 32
    group = lane_group(chunk, width)
    sign = 1.0 - 2.0 * (lax.broadcasted_iota(jnp.int32, (chunk, LANES), 0) % 2).astype(jnp.float32)

    def read(start, tile):
        lanes = slice(tile * LANES, (tile + 1) * LANES)
        return (
            spec[pl.ds(pl.multiple_of(start, chunk), chunk), lanes],
            spec[pl.ds(pl.multiple_of(rows + start, chunk), chunk), lanes],
        )

    def shifted(blocks, tile, places):
        turned = pltpu.roll(blocks[tile], places * width, 1)
        before = pltpu.roll(blocks[tile - 1], places * width, 1) if tile > 0 else 0.0
        return jnp.where(group >= places, turned, before)

    for share in range(shares):
        exchange(send_h, recv_h, h_send, h_recv, share, arrived)
        for tile in range(share_tiles):
            taps = unpack(recv_h, share, tile).astype(jnp.bfloat16)
            spec[:, tile * LANES : (tile + 1) * LANES] = dot(table[0], taps) + dot(table[1], taps)

        def spread_chunk(index, carry):
            begin = index * chunk
            at = pl.ds(pl.multiple_of(begin, chunk), chunk)
            loaded = [read(begin, tile) for tile in range(share_tiles)]
            real = [pair[0] for pair in loaded]
            imag = [pair[1] for pair in loaded]
            for tile in range(share_tiles):
                both = (
                    real[tile] - sign * shifted(imag, tile, 1),
                    imag[tile] + sign * shifted(real, tile, 1),
                )
                for part, block in enumerate(both):
                    for k, wide in enumerate(spread_groups(block, width)):
                        spread[share, k, tile, part, at, :] = wide
            return carry

        lax.fori_loop(0, rows // chunk, spread_chunk, 0)

    for share in range(shares):
        exchange(send_g, recv_g, g_send, g_recv, share, arrived)
        for tile in range(share_tiles):
            high, low = halves(unpack(recv_g, share, tile))
            spec[:, tile * LANES : (tile + 1) * LANES] = (
                dot(table[0], high) + dot(table[1], high) + dot(table[0], low)
            )

        def product_chunk(index, carry):
            begin = index * chunk
            at = pl.ds(pl.multiple_of(begin, chunk), chunk)
            also = pl.ds(pl.multiple_of(rows + begin, chunk), chunk)
            loaded = [read(begin, tile) for tile in range(share_tiles)]
            real = [pair[0] for pair in loaded]
            imag = [pair[1] for pair in loaded]

            def step(k, sums):
                sums = list(sums)
                moved_real = [shifted(real, tile, k) for tile in range(share_tiles)]
                moved_imag = [shifted(imag, tile, k) for tile in range(share_tiles)]
                for apart in range(share_tiles):
                    kr = spread[share, k, apart, 0, at, :]
                    ki = spread[share, k, apart, 1, at, :]
                    for tile in range(apart, share_tiles):
                        xr, xi = moved_real[tile - apart], moved_imag[tile - apart]
                        sums[2 * tile] = sums[2 * tile] + (xr * kr - xi * ki)
                        sums[2 * tile + 1] = sums[2 * tile + 1] + (xr * ki + xi * kr)
                return tuple(sums)

            zero = jnp.zeros((chunk, LANES), jnp.float32)
            sums = loop(0, count, step, (zero,) * (2 * share_tiles))
            for tile in range(share_tiles):
                lanes = slice(tile * LANES, (tile + 1) * LANES)
                for where, total in ((at, sums[2 * tile]), (also, sums[2 * tile + 1])):
                    high, low = halves(total)
                    prod[0, where, lanes] = high
                    prod[1, where, lanes] = low
            return carry

        lax.fori_loop(0, rows // chunk, product_chunk, 0)

        for tile in range(share_tiles):
            lanes = slice(tile * LANES, (tile + 1) * LANES)
            high, low = prod[0, :, lanes], prod[1, :, lanes]
            long_rows = (
                dot(back_table[0], high) + dot(back_table[1], high) + dot(back_table[0], low)
            )
            parts = [long_rows[q * piece : (q + 1) * piece] for q in range(count)]
            for q, part in enumerate(exchange_groups(parts, width)):
                send_r[share, tile * count + q] = part
        exchange(send_r, recv_r, r_send, r_recv, share, start)
        keep_own(send_r, recv_r, share)

    for tile in range(tiles):
        for q in range(count):
            r, c = q * piece, tile * LANES
            at, lanes = slice(r, r + piece), slice(c, c + LANES)
            first = short(1, r, c)
            ext[0, at, lanes] = first
            kept[at, lanes] = skip[:, lanes] * kept[at, lanes] * first
    for share in range(shares):
        exchange(send_h, recv_h, h_send, h_recv, share, left)
        exchange(send_g, recv_g, g_send, g_recv, share, left)
    for share in range(shares):
        exchange(send_r, recv_r, r_send, r_recv, share, arrived)
    for tile in range(tiles):
        lanes = slice(tile * LANES, (tile + 1) * LANES)
        parts = []
        for q in range(count):
            device, share = place_of(tile, q)
            parts.append(recv_r[share, device])
        for q, part in enumerate(exchange_groups(parts, width)):
            at = slice(q * piece, (q + 1) * piece)
            out[at, lanes] = (ext[0, at, lanes] * part + kept[at, lanes]).astype(out.dtype)
    for share in range(shares):
        exchange(send_r, recv_r, r_send, r_recv, share, left)


def body(gate_stream, outer_stream, value_stream, short_weight, long_filter, skip_gain):
    devices = lax.axis_size("ctx")
    rows, channels = gate_stream.shape
    tiles = channels // LANES
    shares = 2
    while shares > 1 and (tiles % shares or rows * channels // (devices * shares * LANES) < 16):
        shares -= 1
    width = channels // (devices * shares)
    count = LANES // width
    piece = rows // count
    share_tiles = tiles // shares
    table = transform_table(rows)
    filter_type = jnp.bfloat16 if piece % 16 == 0 else jnp.float32
    full = pltpu.VMEM((shares, devices, piece, LANES), jnp.float32)
    part = pltpu.VMEM((shares, devices, piece, LANES), filter_type)
    many = pltpu.SemaphoreType.DMA((shares, devices))
    operands = (
        gate_stream, outer_stream, value_stream, short_weight, long_filter, skip_gain[None, :],
        jnp.asarray(split(table)), jnp.asarray(split(table.T / rows)),
    )
    return pl.pallas_call(
        functools.partial(kernel, devices, shares),
        out_shape=jax.ShapeDtypeStruct((rows, channels), jnp.bfloat16),
        in_specs=[pl.BlockSpec(memory_space=pltpu.HBM)] * len(operands),
        out_specs=pl.BlockSpec(memory_space=pltpu.VMEM),
        scratch_shapes=[
            *(pltpu.VMEM(each.shape, each.dtype) for each in operands),
            pltpu.VMEM((3, RIM + rows, channels), jnp.float32),
            pltpu.VMEM((3, RIM, channels), jnp.float32),
            pltpu.VMEM((3, RIM, channels), jnp.float32),
            part, part, full, full, full, full,
            pltpu.VMEM((2 * rows, share_tiles * LANES), jnp.float32),
            pltpu.VMEM((shares, count, share_tiles, 2, rows, LANES), jnp.float32),
            pltpu.VMEM((2, 2 * rows, share_tiles * LANES), jnp.bfloat16),
            pltpu.VMEM((rows, channels), jnp.float32),
            pltpu.SemaphoreType.DMA((len(operands),)),
            pltpu.SemaphoreType.DMA,
            pltpu.SemaphoreType.DMA,
            many, many, many, many, many, many,
        ],
        compiler_params=pltpu.CompilerParams(
            collective_id=0, has_side_effects=True, vmem_limit_bytes=63 * 1024 * 1024
        ),
        cost_estimate=pl.CostEstimate(
            flops=2 * 16 * rows * rows * channels, bytes_accessed=4 * rows * channels, transcendentals=0
        ),
    )(*operands)


def solution(mesh):
    placed = (
        P(("groups", "ctx"), "ch"),
        P(("groups", "ctx"), "ch"),
        P(("groups", "ctx"), "ch"),
        P(None, None, "ch"),
        P("ctx", "ch"),
        P("ch"),
    )
    return jax.shard_map(
        body, mesh=mesh, in_specs=placed, out_specs=P(("groups", "ctx"), "ch"), check_vma=False
    )
```

```python
import functools

import jax
import jax.numpy as jnp
import numpy as np
from jax import lax
from jax.experimental import pallas as pl
from jax.experimental.pallas import tpu as pltpu
from jax.sharding import PartitionSpec as P

LANES = 128
RIM = 8


def loop(begin, end, step, carry):
    if end - begin <= 8:
        for i in range(begin, end):
            carry = step(i, carry)
        return carry
    return lax.fori_loop(begin, end, step, carry)


def transform_table(rows):
    freq = np.arange(rows)[:, None]
    time = np.arange(rows)[None, :]
    phase = ((2 * freq + 1) * time % (4 * rows)) * (np.pi / (2 * rows))
    return np.concatenate([np.cos(phase), -np.sin(phase)], axis=0)


def split(table):
    table = np.asarray(table, np.float32)
    high = table.astype(jnp.bfloat16)
    low = (table - high.astype(np.float32)).astype(jnp.bfloat16)
    return np.stack([high, low])


def halves(value):
    high = value.astype(jnp.bfloat16)
    low = (value - high.astype(jnp.float32)).astype(jnp.bfloat16)
    return high, low


def dot(a, b):
    return jnp.dot(a, b, preferred_element_type=jnp.float32)


def lane_group(rows, width):
    return lax.broadcasted_iota(jnp.int32, (rows, LANES), 1) // width


def exchange_groups(parts, width):
    parts = list(parts)
    count = LANES // width
    group = lane_group(parts[0].shape[0], width)
    span = 1
    while span < count:
        keep = (group & span) == 0
        for q in range(count):
            if q & span == 0:
                low, high = parts[q], parts[q | span]
                parts[q] = jnp.where(keep, low, pltpu.roll(high, span * width, 1))
                parts[q | span] = jnp.where(keep, pltpu.roll(low, LANES - span * width, 1), high)
        span *= 2
    return parts


def spread_groups(block, width):
    count = LANES // width
    group = lane_group(block.shape[0], width)
    result = [block]
    span = count // 2
    while span:
        keep = (group & span) == 0
        wider = []
        for each in result:
            turned = pltpu.roll(each, span * width, 1)
            wider += [jnp.where(keep, each, turned), jnp.where(keep, turned, each)]
        result = wider
        span //= 2
    return result


def kernel(
    devices, groups, shares, mirrored, gate_hbm, outer_hbm, value_hbm, weight_hbm, filt_hbm, skip_hbm,
    table_hbm, back_hbm, out,
    gate, outer, value, weight, filt, skip, table, back_table,
    ext, rim, send_h, recv_h, send_g, recv_g, send_r, recv_r, spec, spread, prod, kept, factor,
    load_sem, rim_send, rim_recv, h_send, h_recv, m_send, m_recv, g_send, g_recv, r_send, r_recv,
):
    rows, channels = gate.shape
    width = channels // (devices * shares)
    count = LANES // width
    piece = rows // count
    tiles = channels // LANES
    share_tiles = tiles // shares
    me = lax.axis_index("ctx")
    mine = lax.axis_index("groups")

    def partner(distance):
        return lax.rem(me + distance, devices)

    barrier = pltpu.get_barrier_semaphore()

    def greet(distance, carry):
        pl.semaphore_signal(
            barrier, inc=1, device_id={"ctx": partner(distance)}, device_id_type=pl.DeviceIdType.MESH
        )
        return carry

    loop(1, devices, greet, 0)
    peers = [
        {"groups": lax.rem(mine + distance, groups), "ctx": me}
        for distance in range(1, groups if mirrored else 1)
    ]
    for peer in peers:
        pl.semaphore_signal(barrier, inc=1, device_id=peer, device_id_type=pl.DeviceIdType.MESH)

    pairs = (
        (filt_hbm, filt), (gate_hbm, gate), (value_hbm, value), (weight_hbm, weight),
        (outer_hbm, outer), (skip_hbm, skip), (table_hbm, table), (back_hbm, back_table),
    )
    loads = [pltpu.make_async_copy(src, dst, load_sem.at[i]) for i, (src, dst) in enumerate(pairs)]
    for load in loads:
        load.start()

    def lanes_of(share, tile):
        return pl.ds(pl.multiple_of((share * share_tiles + tile) * LANES, LANES), LANES)

    def pack(source, send, share):
        for tile in range(share_tiles):
            lanes = lanes_of(share, tile)
            parts = [source(q * piece, lanes) for q in range(count)]
            for q, part in enumerate(exchange_groups(parts, width)):
                send[share, tile * count + q] = part.astype(send.dtype)

    def unpack(recv, share, tile):
        parts = [recv[share, tile * count + q].astype(jnp.float32) for q in range(count)]
        return exchange_groups(parts, width)

    def exchange(send, recv, send_sem, recv_sem, share, act):
        def step(distance, carry):
            copy = pltpu.make_async_remote_copy(
                src_ref=send.at[share, partner(distance)],
                dst_ref=recv.at[share, me],
                send_sem=send_sem.at[share, distance],
                recv_sem=recv_sem.at[share, distance],
                device_id={"ctx": partner(distance)},
                device_id_type=pl.DeviceIdType.MESH,
            )
            act(copy)
            return carry

        loop(1, devices, step, 0)

    def keep_own(send, recv, share):
        recv[share, pl.ds(me, 1)] = send[share, pl.ds(me, 1)]

    def start(copy):
        copy.start()

    def arrived(copy):
        copy.wait_recv()

    def left(copy):
        copy.wait_send()

    pl.semaphore_wait(barrier, devices - 1 + len(peers))
    rim_copies = [
        pltpu.make_async_remote_copy(
            src_ref=stream.at[rows - rim.shape[1] :],
            dst_ref=rim.at[i],
            send_sem=rim_send.at[i],
            recv_sem=rim_recv.at[i],
            device_id={"ctx": partner(1)},
            device_id_type=pl.DeviceIdType.MESH,
        )
        for i, stream in enumerate((gate_hbm, outer_hbm, value_hbm))
    ]
    for i in (0, 2, 1):
        rim_copies[i].start()

    order = [lax.rem(mine + i, shares) for i in range(shares)] if mirrored else range(shares)
    loads[0].wait()
    for share in order[:1] if mirrored else order:
        pack(lambda r, lanes: filt[r : r + piece, lanes].astype(jnp.float32), send_h, share)
        exchange(send_h, recv_h, h_send, h_recv, share, start)
        keep_own(send_h, recv_h, share)

    def extend(i, stream):
        ext[i, RIM:, :] = stream[...].astype(jnp.float32)
        rim_copies[i].wait()
        last = rim[i].astype(jnp.float32)[rim.shape[1] - RIM :]
        ext[i, :RIM, :] = jnp.where(me > 0, last, 0.0)

    def short(i, r, lanes):
        taps = weight[i, :, lanes].astype(jnp.float32)
        total = None
        for offset in range(taps.shape[0]):
            begin = r + RIM - offset
            term = taps[offset : offset + 1] * ext[i, begin : begin + piece, lanes]
            total = term if total is None else total + term
        return total

    def gated(r, lanes):
        result = short(0, r, lanes) * short(2, r, lanes)
        kept[r : r + piece, lanes] = result
        return result

    for load in loads[1:4]:
        load.wait()
    extend(0, gate)
    extend(2, value)
    for share in order:
        pack(gated, send_g, share)
        exchange(send_g, recv_g, g_send, g_recv, share, start)
        keep_own(send_g, recv_g, share)
    for load in loads[4:]:
        load.wait()

    chunk = 32
    group = lane_group(chunk, width)
    sign = 1.0 - 2.0 * (lax.broadcasted_iota(jnp.int32, (chunk, LANES), 0) % 2).astype(jnp.float32)

    def read(start, tile):
        lanes = slice(tile * LANES, (tile + 1) * LANES)
        return (
            spec[pl.ds(pl.multiple_of(start, chunk), chunk), lanes],
            spec[pl.ds(pl.multiple_of(rows + start, chunk), chunk), lanes],
        )

    def shifted(blocks, tile, places):
        turned = pltpu.roll(blocks[tile], places * width, 1)
        before = pltpu.roll(blocks[tile - 1], places * width, 1) if tile > 0 else 0.0
        return jnp.where(group >= places, turned, before)

    def mirror(distance, share):
        return pltpu.make_async_remote_copy(
            src_ref=recv_h.at[share],
            dst_ref=recv_h.at[share],
            send_sem=m_send.at[distance],
            recv_sem=m_recv.at[distance],
            device_id=peers[distance],
            device_id_type=pl.DeviceIdType.MESH,
        )

    for turn, share in enumerate(order):
        if turn == 0 or not mirrored:
            exchange(send_h, recv_h, h_send, h_recv, share, arrived)
            for distance in range(len(peers)):
                mirror(distance, share).start()
        else:
            mirror(len(peers) - turn, share).wait_recv()
        for tile in range(share_tiles):
            taps = jnp.concatenate(unpack(recv_h, share, tile), axis=0).astype(jnp.bfloat16)
            spec[:, tile * LANES : (tile + 1) * LANES] = dot(table[0], taps) + dot(table[1], taps)

        def spread_chunk(index, carry):
            begin = index * chunk
            at = pl.ds(pl.multiple_of(begin, chunk), chunk)
            loaded = [read(begin, tile) for tile in range(share_tiles)]
            real = [pair[0] for pair in loaded]
            imag = [pair[1] for pair in loaded]
            for tile in range(share_tiles):
                both = (
                    real[tile] - sign * shifted(imag, tile, 1),
                    imag[tile] + sign * shifted(real, tile, 1),
                )
                for part, block in enumerate(both):
                    for k, wide in enumerate(spread_groups(block, width)):
                        spread[share, k, tile, part, at, :] = wide
            return carry

        lax.fori_loop(0, rows // chunk, spread_chunk, 0)

    extend(1, outer)
    for tile in range(tiles):
        lanes = slice(tile * LANES, (tile + 1) * LANES)
        for q in range(count):
            at = slice(q * piece, (q + 1) * piece)
            first = short(1, q * piece, lanes)
            factor[at, lanes] = first
            kept[at, lanes] = skip[:, lanes] * kept[at, lanes] * first

    for share in order:
        exchange(send_g, recv_g, g_send, g_recv, share, arrived)
        for tile in range(share_tiles):
            high, low = halves(jnp.concatenate(unpack(recv_g, share, tile), axis=0))
            spec[:, tile * LANES : (tile + 1) * LANES] = (
                dot(table[0], high) + dot(table[1], high) + dot(table[0], low)
            )

        def product_chunk(index, carry):
            begin = index * chunk
            at = pl.ds(pl.multiple_of(begin, chunk), chunk)
            also = pl.ds(pl.multiple_of(rows + begin, chunk), chunk)
            loaded = [read(begin, tile) for tile in range(share_tiles)]
            real = [pair[0] for pair in loaded]
            imag = [pair[1] for pair in loaded]

            def step(k, sums):
                sums = list(sums)
                moved_real = [shifted(real, tile, k) for tile in range(share_tiles)]
                moved_imag = [shifted(imag, tile, k) for tile in range(share_tiles)]
                for apart in range(share_tiles):
                    kr = spread[share, k, apart, 0, at, :]
                    ki = spread[share, k, apart, 1, at, :]
                    for tile in range(apart, share_tiles):
                        xr, xi = moved_real[tile - apart], moved_imag[tile - apart]
                        sums[2 * tile] = sums[2 * tile] + (xr * kr - xi * ki)
                        sums[2 * tile + 1] = sums[2 * tile + 1] + (xr * ki + xi * kr)
                return tuple(sums)

            zero = jnp.zeros((chunk, LANES), jnp.float32)
            sums = loop(0, count, step, (zero,) * (2 * share_tiles))
            for tile in range(share_tiles):
                lanes = slice(tile * LANES, (tile + 1) * LANES)
                for where, total in ((at, sums[2 * tile]), (also, sums[2 * tile + 1])):
                    high, low = halves(total)
                    prod[0, where, lanes] = high
                    prod[1, where, lanes] = low
            return carry

        lax.fori_loop(0, rows // chunk, product_chunk, 0)

        for tile in range(share_tiles):
            lanes = slice(tile * LANES, (tile + 1) * LANES)
            high, low = prod[0, :, lanes], prod[1, :, lanes]
            long_rows = (
                dot(back_table[0], high) + dot(back_table[1], high) + dot(back_table[0], low)
            )
            parts = [long_rows[q * piece : (q + 1) * piece] for q in range(count)]
            for q, part in enumerate(exchange_groups(parts, width)):
                send_r[share, tile * count + q] = part
        exchange(send_r, recv_r, r_send, r_recv, share, start)
        keep_own(send_r, recv_r, share)

    for share in order:
        exchange(send_r, recv_r, r_send, r_recv, share, arrived)
        for tile in range(share_tiles):
            lanes = lanes_of(share, tile)
            for q, part in enumerate(unpack(recv_r, share, tile)):
                at = slice(q * piece, (q + 1) * piece)
                out[at, lanes] = (factor[at, lanes] * part + kept[at, lanes]).astype(out.dtype)
    for share in order[:1] if mirrored else order:
        exchange(send_h, recv_h, h_send, h_recv, share, left)
        for distance in range(len(peers)):
            mirror(distance, share).wait_send()
    for share in order:
        exchange(send_g, recv_g, g_send, g_recv, share, left)
        exchange(send_r, recv_r, r_send, r_recv, share, left)


def body(gate_stream, outer_stream, value_stream, short_weight, long_filter, skip_gain):
    devices, groups = lax.axis_size("ctx"), lax.axis_size("groups")
    rows, channels = gate_stream.shape
    tiles = channels // LANES
    shares = 2
    while shares > 1 and (tiles % shares or rows * channels // (devices * shares * LANES) < 16):
        shares -= 1
    width = channels // (devices * shares)
    count = LANES // width
    piece = rows // count
    share_tiles = tiles // shares
    table = transform_table(rows)
    filter_type = jnp.bfloat16 if piece % 16 == 0 else jnp.float32
    full = pltpu.VMEM((shares, devices, piece, LANES), jnp.float32)
    part = pltpu.VMEM((shares, devices, piece, LANES), filter_type)
    many = pltpu.SemaphoreType.DMA((shares, devices))
    operands = (
        gate_stream, outer_stream, value_stream, short_weight, long_filter, skip_gain[None, :],
        jnp.asarray(split(table)), jnp.asarray(split(table.T / rows)),
    )
    return pl.pallas_call(
        functools.partial(kernel, devices, groups, shares, shares == groups > 1),
        out_shape=jax.ShapeDtypeStruct((rows, channels), jnp.bfloat16),
        in_specs=[pl.BlockSpec(memory_space=pltpu.HBM)] * len(operands),
        out_specs=pl.BlockSpec(memory_space=pltpu.VMEM),
        scratch_shapes=[
            *(pltpu.VMEM(each.shape, each.dtype) for each in operands),
            pltpu.VMEM((3, RIM + rows, channels), jnp.float32),
            pltpu.VMEM((3, 16, channels), jnp.bfloat16),
            part, part, full, full, full, full,
            pltpu.VMEM((2 * rows, share_tiles * LANES), jnp.float32),
            pltpu.VMEM((shares, count, share_tiles, 2, rows, LANES), jnp.float32),
            pltpu.VMEM((2, 2 * rows, share_tiles * LANES), jnp.bfloat16),
            pltpu.VMEM((rows, channels), jnp.float32),
            pltpu.VMEM((rows, channels), jnp.float32),
            pltpu.SemaphoreType.DMA((len(operands),)),
            pltpu.SemaphoreType.DMA((3,)),
            pltpu.SemaphoreType.DMA((3,)),
            many, many,
            pltpu.SemaphoreType.DMA((groups,)),
            pltpu.SemaphoreType.DMA((groups,)),
            many, many, many, many,
        ],
        compiler_params=pltpu.CompilerParams(
            collective_id=0, has_side_effects=True, vmem_limit_bytes=64 * 1024 * 1024 - 320 * 1024
        ),
        cost_estimate=pl.CostEstimate(
            flops=2 * 16 * rows * rows * channels, bytes_accessed=4 * rows * channels, transcendentals=0
        ),
    )(*operands)


def solution(mesh):
    placed = (
        P(("groups", "ctx"), "ch"),
        P(("groups", "ctx"), "ch"),
        P(("groups", "ctx"), "ch"),
        P(None, None, "ch"),
        P("ctx", "ch"),
        P("ch"),
    )
    return jax.shard_map(
        body, mesh=mesh, in_specs=placed, out_specs=P(("groups", "ctx"), "ch"), check_vma=False
    )
```

```python
import functools

import jax
import jax.numpy as jnp
import numpy as np
from jax import lax
from jax.experimental import pallas as pl
from jax.experimental.pallas import tpu as pltpu
from jax.sharding import PartitionSpec as P

LANES = 128
RIM = 8


def loop(begin, end, step, carry):
    if end - begin <= 8:
        for i in range(begin, end):
            carry = step(i, carry)
        return carry
    return lax.fori_loop(begin, end, step, carry)


def transform_table(rows):
    freq = np.arange(rows)[:, None]
    time = np.arange(rows)[None, :]
    phase = ((2 * freq + 1) * time % (4 * rows)) * (np.pi / (2 * rows))
    return np.concatenate([np.cos(phase), -np.sin(phase)], axis=0)


def split(table):
    table = np.asarray(table, np.float32)
    high = table.astype(jnp.bfloat16)
    low = (table - high.astype(np.float32)).astype(jnp.bfloat16)
    return np.stack([high, low])


def halves(value):
    high = value.astype(jnp.bfloat16)
    low = (value - high.astype(jnp.float32)).astype(jnp.bfloat16)
    return high, low


def dot(a, b):
    return jnp.dot(a, b, preferred_element_type=jnp.float32)


def lane_group(rows, width):
    return lax.broadcasted_iota(jnp.int32, (rows, LANES), 1) // width


def exchange_groups(parts, width):
    parts = list(parts)
    count = LANES // width
    group = lane_group(parts[0].shape[0], width)
    span = 1
    while span < count:
        keep = (group & span) == 0
        for q in range(count):
            if q & span == 0:
                low, high = parts[q], parts[q | span]
                parts[q] = jnp.where(keep, low, pltpu.roll(high, span * width, 1))
                parts[q | span] = jnp.where(keep, pltpu.roll(low, LANES - span * width, 1), high)
        span *= 2
    return parts


def spread_groups(block, width):
    count = LANES // width
    group = lane_group(block.shape[0], width)
    result = [block]
    span = count // 2
    while span:
        keep = (group & span) == 0
        wider = []
        for each in result:
            turned = pltpu.roll(each, span * width, 1)
            wider += [jnp.where(keep, each, turned), jnp.where(keep, turned, each)]
        result = wider
        span //= 2
    return result


def kernel(
    devices, shares, gate_hbm, outer_hbm, value_hbm, weight_hbm, filt_hbm, skip_hbm,
    table_hbm, back_hbm, out_hbm,
    gate, outer, value, weight, filt, skip, table, back_table,
    ext, rim, send_h, recv_h, send_g, recv_g, send_r, recv_r, spec, spec_h, spread, prod, kept, factor, out,
    load_sem, out_sem, rim_send, rim_recv, h_send, h_recv, g_send, g_recv, r_send, r_recv,
):
    rows, channels = gate.shape
    width = channels // (devices * shares)
    count = LANES // width
    piece = rows // count
    tiles = channels // LANES
    share_tiles = tiles // shares
    wide = share_tiles * LANES
    me = lax.axis_index("ctx")

    def partner(distance):
        return lax.rem(me + distance, devices)

    barrier = pltpu.get_barrier_semaphore()

    def greet(distance, carry):
        pl.semaphore_signal(
            barrier, inc=1, device_id={"ctx": partner(distance)}, device_id_type=pl.DeviceIdType.MESH
        )
        return carry

    loop(1, devices, greet, 0)
    pairs = (
        (filt_hbm, filt), (gate_hbm, gate), (value_hbm, value), (weight_hbm, weight),
        (outer_hbm, outer), (skip_hbm, skip), (table_hbm, table), (back_hbm, back_table),
    )
    loads = [pltpu.make_async_copy(src, dst, load_sem.at[i]) for i, (src, dst) in enumerate(pairs)]
    for load in loads:
        load.start()

    def lanes_of(share, tile):
        begin = (share * share_tiles + tile) * LANES
        return slice(begin, begin + LANES)

    def pack(source, share, store):
        for tile in range(share_tiles):
            lanes = lanes_of(share, tile)
            parts = [source(q * piece, piece, lanes) for q in range(count)]
            for q, part in enumerate(exchange_groups(parts, width)):
                store(share, tile * count + q, part)

    def unpack(read, tile):
        parts = [read(tile * count + q).astype(jnp.float32) for q in range(count)]
        return exchange_groups(parts, width)

    def exchange(sent, landed, send_sem, recv_sem, act):
        def step(distance, carry):
            copy = pltpu.make_async_remote_copy(
                src_ref=sent(partner(distance)),
                dst_ref=landed(me),
                send_sem=send_sem.at[distance],
                recv_sem=recv_sem.at[distance],
                device_id={"ctx": partner(distance)},
                device_id_type=pl.DeviceIdType.MESH,
            )
            act(copy)
            return carry

        loop(1, devices, step, 0)

    def filters(act):
        exchange(lambda i: send_h.at[i], lambda i: recv_h.at[i], h_send, h_recv, act)

    def values(share, act):
        exchange(
            lambda i: send_g.at[share, i], lambda i: recv_g.at[share, i],
            g_send.at[share], g_recv.at[share], act,
        )

    def results(share, act):
        exchange(
            lambda i: send_r.at[share, i], lambda i: recv_r.at[share, i],
            r_send.at[share], r_recv.at[share], act,
        )

    def start(copy):
        copy.start()

    def arrived(copy):
        copy.wait_recv()

    def left(copy):
        copy.wait_send()

    pl.semaphore_wait(barrier, devices - 1)
    rim_copies = [
        pltpu.make_async_remote_copy(
            src_ref=stream.at[rows - rim.shape[1] :],
            dst_ref=rim.at[i],
            send_sem=rim_send.at[i],
            recv_sem=rim_recv.at[i],
            device_id={"ctx": partner(1)},
            device_id_type=pl.DeviceIdType.MESH,
        )
        for i, stream in enumerate((gate_hbm, outer_hbm, value_hbm))
    ]
    for i in (0, 2, 1):
        rim_copies[i].start()

    def store_filter(share, device, part):
        send_h[device, share] = part.astype(send_h.dtype)

    def store_value(share, device, part):
        send_g[share, device] = part

    loads[0].wait()
    for share in range(shares):
        pack(lambda r, n, lanes: filt[r : r + n, lanes].astype(jnp.float32), share, store_filter)
    filters(start)

    def short(i, r, n, lanes):
        taps = weight[i, :, lanes].astype(jnp.float32)
        total = None
        for offset in range(taps.shape[0]):
            begin = r + RIM - offset
            term = taps[offset : offset + 1] * ext[i, begin : begin + n, lanes]
            total = term if total is None else total + term
        return total

    def gated(r, n, lanes):
        result = short(0, r, n, lanes) * short(2, r, n, lanes)
        kept[r : r + n, lanes] = result
        return result

    ext[:, :RIM, :] = jnp.zeros((3, RIM, channels), jnp.float32)
    for load in loads[1:4]:
        load.wait()
    ext[0, RIM:, :] = gate[...].astype(jnp.float32)
    ext[2, RIM:, :] = value[...].astype(jnp.float32)
    for share in range(shares):
        pack(gated, share, store_value)
    for i in (0, 2):
        rim_copies[i].wait()
        last = rim[i].astype(jnp.float32)[rim.shape[1] - RIM :]
        ext[i, :RIM, :] = jnp.where(me > 0, last, 0.0)
    first_lanes = lane_group(RIM, width) == 0
    for share in range(shares):
        for tile in range(share_tiles):
            block = gated(0, RIM, lanes_of(share, tile))
            for q in range(count):
                device = tile * count + q
                moved = pltpu.roll(block, (LANES - q * width) % LANES, 1)
                send_g[share, device, :RIM] = jnp.where(
                    first_lanes, moved, send_g[share, device, :RIM]
                )
        values(share, start)
    for share in range(shares):
        recv_g[share, pl.ds(me, 1)] = send_g[share, pl.ds(me, 1)]
    recv_h[pl.ds(me, 1)] = send_h[pl.ds(me, 1)]
    for load in loads[4:]:
        load.wait()

    rim_copies[1].wait()
    ext[1, :RIM, :] = jnp.where(me > 0, rim[1].astype(jnp.float32)[rim.shape[1] - RIM :], 0.0)
    ext[1, RIM:, :] = outer[...].astype(jnp.float32)
    for tile in range(tiles):
        lanes = slice(tile * LANES, (tile + 1) * LANES)
        for q in range(count):
            at = slice(q * piece, (q + 1) * piece)
            first = short(1, q * piece, piece, lanes)
            factor[at, lanes] = first
            kept[at, lanes] = skip[:, lanes] * kept[at, lanes] * first

    chunk = 32
    group = lane_group(chunk, width)
    sign = 1.0 - 2.0 * (lax.broadcasted_iota(jnp.int32, (chunk, LANES), 0) % 2).astype(jnp.float32)

    def read(ref, begin, tile):
        lanes = slice(tile * LANES, (tile + 1) * LANES)
        return (
            ref[pl.ds(pl.multiple_of(begin, chunk), chunk), lanes],
            ref[pl.ds(pl.multiple_of(rows + begin, chunk), chunk), lanes],
        )

    def shifted(blocks, tile, places):
        turned = pltpu.roll(blocks[tile], places * width, 1)
        before = pltpu.roll(blocks[tile - 1], places * width, 1) if tile > 0 else 0.0
        return jnp.where(group >= places, turned, before)

    filters(arrived)
    taps = jnp.concatenate(
        [
            jnp.concatenate(unpack(lambda i: recv_h[i, share], tile), axis=0)
            for share in range(shares)
            for tile in range(share_tiles)
        ],
        axis=1,
    ).astype(jnp.bfloat16)
    spec_h[...] = dot(table[0], taps) + dot(table[1], taps)
    for share in range(shares):

        def spread_chunk(index, carry):
            begin = index * chunk
            at = pl.ds(pl.multiple_of(begin, chunk), chunk)
            loaded = [
                read(spec_h, begin, share * share_tiles + tile) for tile in range(share_tiles)
            ]
            real = [pair[0] for pair in loaded]
            imag = [pair[1] for pair in loaded]
            for tile in range(share_tiles):
                both = (
                    real[tile] - sign * shifted(imag, tile, 1),
                    imag[tile] + sign * shifted(real, tile, 1),
                )
                for part, block in enumerate(both):
                    for k, wide in enumerate(spread_groups(block, width)):
                        spread[share, k, tile, part, at, :] = wide
            return carry

        lax.fori_loop(0, rows // chunk, spread_chunk, 0)

    for share in range(shares):
        values(share, arrived)
        block = jnp.concatenate(
            [
                jnp.concatenate(unpack(lambda i: recv_g[share, i], tile), axis=0)
                for tile in range(share_tiles)
            ],
            axis=1,
        )
        high, low = halves(block)
        both = dot(table[0], jnp.concatenate([high, low], axis=1))
        spec[...] = both[:, :wide] + both[:, wide:] + dot(table[1], high)

        def product_chunk(index, carry):
            begin = index * chunk
            at = pl.ds(pl.multiple_of(begin, chunk), chunk)
            also = pl.ds(pl.multiple_of(rows + begin, chunk), chunk)
            loaded = [read(spec, begin, tile) for tile in range(share_tiles)]
            real = [pair[0] for pair in loaded]
            imag = [pair[1] for pair in loaded]

            def step(k, sums):
                sums = list(sums)
                moved_real = [shifted(real, tile, k) for tile in range(share_tiles)]
                moved_imag = [shifted(imag, tile, k) for tile in range(share_tiles)]
                for apart in range(share_tiles):
                    kr = spread[share, k, apart, 0, at, :]
                    ki = spread[share, k, apart, 1, at, :]
                    for tile in range(apart, share_tiles):
                        xr, xi = moved_real[tile - apart], moved_imag[tile - apart]
                        sums[2 * tile] = sums[2 * tile] + (xr * kr - xi * ki)
                        sums[2 * tile + 1] = sums[2 * tile + 1] + (xr * ki + xi * kr)
                return tuple(sums)

            zero = jnp.zeros((chunk, LANES), jnp.float32)
            sums = loop(0, count, step, (zero,) * (2 * share_tiles))
            for tile in range(share_tiles):
                lanes = slice(tile * LANES, (tile + 1) * LANES)
                for where, total in ((at, sums[2 * tile]), (also, sums[2 * tile + 1])):
                    high, low = halves(total)
                    prod[where, lanes] = high
                    prod[where, slice(wide + lanes.start, wide + lanes.stop)] = low
            return carry

        lax.fori_loop(0, rows // chunk, product_chunk, 0)

        both = dot(back_table[0], prod[...])
        long_rows = both[:, :wide] + both[:, wide:] + dot(back_table[1], prod[:, :wide])
        for tile in range(share_tiles):
            lanes = slice(tile * LANES, (tile + 1) * LANES)
            parts = [long_rows[q * piece : (q + 1) * piece, lanes] for q in range(count)]
            for q, part in enumerate(exchange_groups(parts, width)):
                send_r[share, tile * count + q] = part
        results(share, start)
        recv_r[share, pl.ds(me, 1)] = send_r[share, pl.ds(me, 1)]

    leaving = []
    for share in range(shares):
        results(share, arrived)
        for tile in range(share_tiles):
            lanes = lanes_of(share, tile)
            for q, part in enumerate(unpack(lambda i: recv_r[share, i], tile)):
                at = slice(q * piece, (q + 1) * piece)
                out[at, lanes] = (factor[at, lanes] * part + kept[at, lanes]).astype(out.dtype)
        lanes = slice(share * wide, (share + 1) * wide)
        leaving.append(
            pltpu.make_async_copy(out.at[:, lanes], out_hbm.at[:, lanes], out_sem.at[share])
        )
        leaving[-1].start()
    filters(left)
    for share in range(shares):
        values(share, left)
        results(share, left)
    for copy in leaving:
        copy.wait()


def body(gate_stream, outer_stream, value_stream, short_weight, long_filter, skip_gain):
    devices = lax.axis_size("ctx")
    rows, channels = gate_stream.shape
    tiles = channels // LANES
    shares = 2
    while shares > 1 and (tiles % shares or rows * channels // (devices * shares * LANES) < 16):
        shares -= 1
    width = channels // (devices * shares)
    count = LANES // width
    piece = rows // count
    share_tiles = tiles // shares
    table = transform_table(rows)
    filter_type = jnp.bfloat16 if piece % 16 == 0 else jnp.float32
    full = pltpu.VMEM((shares, devices, piece, LANES), jnp.float32)
    part = pltpu.VMEM((devices, shares, piece, LANES), filter_type)
    many = pltpu.SemaphoreType.DMA((shares, devices))
    operands = (
        gate_stream, outer_stream, value_stream, short_weight, long_filter, skip_gain[None, :],
        jnp.asarray(split(table)), jnp.asarray(split(table.T / rows)),
    )
    return pl.pallas_call(
        functools.partial(kernel, devices, shares),
        out_shape=jax.ShapeDtypeStruct((rows, channels), jnp.bfloat16),
        in_specs=[pl.BlockSpec(memory_space=pltpu.HBM)] * len(operands),
        out_specs=pl.BlockSpec(memory_space=pltpu.HBM),
        scratch_shapes=[
            *(pltpu.VMEM(each.shape, each.dtype) for each in operands),
            pltpu.VMEM((3, RIM + rows, channels), jnp.float32),
            pltpu.VMEM((3, 16, channels), jnp.bfloat16),
            part, part, full, full, full, full,
            pltpu.VMEM((2 * rows, share_tiles * LANES), jnp.float32),
            pltpu.VMEM((2 * rows, channels), jnp.float32),
            pltpu.VMEM((shares, count, share_tiles, 2, rows, LANES), jnp.float32),
            pltpu.VMEM((2 * rows, 2 * share_tiles * LANES), jnp.bfloat16),
            pltpu.VMEM((rows, channels), jnp.float32),
            pltpu.VMEM((rows, channels), jnp.float32),
            pltpu.VMEM((rows, channels), jnp.bfloat16),
            pltpu.SemaphoreType.DMA((len(operands),)),
            pltpu.SemaphoreType.DMA((shares,)),
            pltpu.SemaphoreType.DMA((3,)),
            pltpu.SemaphoreType.DMA((3,)),
            pltpu.SemaphoreType.DMA((devices,)),
            pltpu.SemaphoreType.DMA((devices,)),
            many, many, many, many,
        ],
        compiler_params=pltpu.CompilerParams(
            collective_id=0, has_side_effects=True, vmem_limit_bytes=64 * 1024 * 1024 - 320 * 1024
        ),
        cost_estimate=pl.CostEstimate(
            flops=2 * 16 * rows * rows * channels, bytes_accessed=4 * rows * channels, transcendentals=0
        ),
    )(*operands)


def solution(mesh):
    placed = (
        P(("groups", "ctx"), "ch"),
        P(("groups", "ctx"), "ch"),
        P(("groups", "ctx"), "ch"),
        P(None, None, "ch"),
        P("ctx", "ch"),
        P("ch"),
    )
    return jax.shard_map(
        body, mesh=mesh, in_specs=placed, out_specs=P(("groups", "ctx"), "ch"), check_vma=False
    )
```

```python
import functools

import jax
import jax.numpy as jnp
import numpy as np
from jax import lax
from jax.experimental import pallas as pl
from jax.experimental.pallas import tpu as pltpu
from jax.sharding import PartitionSpec as P

LANES = 128
RIM = 8


def loop(begin, end, step, carry):
    if end - begin <= 8:
        for i in range(begin, end):
            carry = step(i, carry)
        return carry
    return lax.fori_loop(begin, end, step, carry)


def transform_table(rows):
    freq = np.arange(rows)[:, None]
    time = np.arange(rows)[None, :]
    phase = ((2 * freq + 1) * time % (4 * rows)) * (np.pi / (2 * rows))
    return np.concatenate([np.cos(phase), -np.sin(phase)], axis=0)


def split(table):
    table = np.asarray(table, np.float32)
    high = table.astype(jnp.bfloat16)
    low = (table - high.astype(np.float32)).astype(jnp.bfloat16)
    return np.stack([high, low])


def halves(value):
    high = value.astype(jnp.bfloat16)
    low = (value - high.astype(jnp.float32)).astype(jnp.bfloat16)
    return high, low


def dot(a, b):
    return jnp.dot(a, b, preferred_element_type=jnp.float32)


def lane_group(rows, width):
    return lax.broadcasted_iota(jnp.int32, (rows, LANES), 1) // width


def exchange_groups(parts, width):
    parts = list(parts)
    count = LANES // width
    group = lane_group(parts[0].shape[0], width)
    span = 1
    while span < count:
        keep = (group & span) == 0
        for q in range(count):
            if q & span == 0:
                low, high = parts[q], parts[q | span]
                parts[q] = jnp.where(keep, low, pltpu.roll(high, span * width, 1))
                parts[q | span] = jnp.where(keep, pltpu.roll(low, LANES - span * width, 1), high)
        span *= 2
    return parts


def spread_groups(block, width):
    count = LANES // width
    group = lane_group(block.shape[0], width)
    result = [block]
    span = count // 2
    while span:
        keep = (group & span) == 0
        wider = []
        for each in result:
            turned = pltpu.roll(each, span * width, 1)
            wider += [jnp.where(keep, each, turned), jnp.where(keep, turned, each)]
        result = wider
        span //= 2
    return result


def kernel(
    devices, groups, shares, crossed, gate_hbm, outer_hbm, value_hbm, weight_hbm, filt_hbm, skip_hbm,
    table_hbm, back_hbm, out_hbm,
    gate, outer, value, weight, filt, skip, table, back_table,
    ext, rim, send_h, recv_h, send_g, recv_g, send_r, recv_r, spec, spec_h, spread, prod, kept, factor, out,
    load_sem, out_sem, rim_send, rim_recv, h_send, h_recv, g_send, g_recv, r_send, r_recv,
):
    rows, channels = gate.shape
    width = channels // (devices * shares)
    count = LANES // width
    piece = rows // count
    tiles = channels // LANES
    share_tiles = tiles // shares
    wide = share_tiles * LANES
    filters_held = 1 if crossed else shares
    me = lax.axis_index("ctx")
    mine = lax.axis_index("groups")

    def partner(distance):
        return lax.rem(me + distance, devices)

    def ahead(stage):
        return lax.rem(mine + stage, groups) if crossed else stage

    def behind(stage):
        return lax.rem(mine + groups - stage, groups) if crossed else stage

    def distances(stage):
        return 0 if crossed and stage > 0 else 1, devices

    def device_at(group, place):
        return {"groups": group if crossed else mine, "ctx": place}

    barrier = pltpu.get_barrier_semaphore()
    met = 0
    for stage in range(shares if crossed else 1):

        def greet(distance, carry):
            pl.semaphore_signal(
                barrier, inc=1, device_id=device_at(ahead(stage), partner(distance)),
                device_id_type=pl.DeviceIdType.MESH,
            )
            return carry

        loop(*distances(stage), greet, 0)
        met += devices - distances(stage)[0]

    pairs = (
        (filt_hbm, filt), (gate_hbm, gate), (value_hbm, value), (weight_hbm, weight),
        (outer_hbm, outer), (skip_hbm, skip), (table_hbm, table), (back_hbm, back_table),
    )
    loads = [pltpu.make_async_copy(src, dst, load_sem.at[i]) for i, (src, dst) in enumerate(pairs)]
    for load in loads:
        load.start()

    def lanes_of(share, tile):
        begin = (share * share_tiles + tile) * LANES
        return pl.ds(pl.multiple_of(begin, LANES), LANES)

    def pack(source, share, store):
        for tile in range(share_tiles):
            lanes = lanes_of(share, tile)
            parts = [source(q * piece, piece, lanes) for q in range(count)]
            for q, part in enumerate(exchange_groups(parts, width)):
                store(tile * count + q, part)

    def unpack(read, tile):
        parts = [read(tile * count + q).astype(jnp.float32) for q in range(count)]
        return exchange_groups(parts, width)

    def exchange(span, group, sent, landed, send_sem, recv_sem, act):
        def step(distance, carry):
            copy = pltpu.make_async_remote_copy(
                src_ref=sent(partner(distance)),
                dst_ref=landed,
                send_sem=send_sem.at[distance],
                recv_sem=recv_sem.at[distance],
                device_id=device_at(group, partner(distance)),
                device_id_type=pl.DeviceIdType.MESH,
            )
            act(copy)
            return carry

        loop(*span, step, 0)

    def filters(act):
        exchange(
            (1, devices), mine, lambda i: send_h.at[i], recv_h.at[me], h_send, h_recv, act
        )

    def values(stage, act):
        exchange(
            distances(stage), ahead(stage), lambda i: send_g.at[ahead(stage), i],
            recv_g.at[mine if crossed else stage, me], g_send.at[stage], g_recv.at[stage], act,
        )

    def results(stage, act):
        exchange(
            distances(stage), behind(stage), lambda i: send_r.at[behind(stage), i],
            recv_r.at[mine if crossed else stage, me], r_send.at[stage], r_recv.at[stage], act,
        )

    def start(copy):
        copy.start()

    def arrived(copy):
        copy.wait_recv()

    def left(copy):
        copy.wait_send()

    pl.semaphore_wait(barrier, met)
    rim_copies = [
        pltpu.make_async_remote_copy(
            src_ref=stream.at[rows - rim.shape[1] :],
            dst_ref=rim.at[i],
            send_sem=rim_send.at[i],
            recv_sem=rim_recv.at[i],
            device_id={"groups": mine, "ctx": partner(1)},
            device_id_type=pl.DeviceIdType.MESH,
        )
        for i, stream in enumerate((gate_hbm, outer_hbm, value_hbm))
    ]
    for i in (0, 2, 1):
        rim_copies[i].start()

    loads[0].wait()
    for held in range(filters_held):

        def store_filter(device, part):
            send_h[device, held] = part.astype(send_h.dtype)

        pack(
            lambda r, n, lanes: filt[r : r + n, lanes].astype(jnp.float32),
            mine if crossed else held, store_filter,
        )
    filters(start)

    def short(i, r, n, lanes):
        taps = weight[i, :, lanes].astype(jnp.float32)
        total = None
        for offset in range(taps.shape[0]):
            begin = r + RIM - offset
            term = taps[offset : offset + 1] * ext[i, begin : begin + n, lanes]
            total = term if total is None else total + term
        return total

    def gated(r, n, lanes):
        result = short(0, r, n, lanes) * short(2, r, n, lanes)
        kept[r : r + n, lanes] = result
        return result

    ext[:, :RIM, :] = jnp.zeros((3, RIM, channels), jnp.float32)
    for load in loads[1:4]:
        load.wait()
    ext[0, RIM:, :] = gate[...].astype(jnp.float32)
    ext[2, RIM:, :] = value[...].astype(jnp.float32)
    for stage in range(shares):

        def store_value(device, part):
            send_g[ahead(stage), device] = part

        pack(gated, ahead(stage), store_value)
    for i in (0, 2):
        rim_copies[i].wait()
        last = rim[i].astype(jnp.float32)[rim.shape[1] - RIM :]
        ext[i, :RIM, :] = jnp.where(me > 0, last, 0.0)
    first_lanes = lane_group(RIM, width) == 0
    for stage in range(shares):
        share = ahead(stage)
        for tile in range(share_tiles):
            block = gated(0, RIM, lanes_of(share, tile))
            for q in range(count):
                device = tile * count + q
                moved = pltpu.roll(block, (LANES - q * width) % LANES, 1)
                send_g[share, device, :RIM] = jnp.where(
                    first_lanes, moved, send_g[share, device, :RIM]
                )
        values(stage, start)
    for stage in range(1 if crossed else shares):
        recv_g[behind(stage), pl.ds(me, 1)] = send_g[ahead(stage), pl.ds(me, 1)]
    recv_h[pl.ds(me, 1)] = send_h[pl.ds(me, 1)]
    for load in loads[4:]:
        load.wait()

    rim_copies[1].wait()
    ext[1, :RIM, :] = jnp.where(me > 0, rim[1].astype(jnp.float32)[rim.shape[1] - RIM :], 0.0)
    ext[1, RIM:, :] = outer[...].astype(jnp.float32)
    for tile in range(tiles):
        lanes = slice(tile * LANES, (tile + 1) * LANES)
        for q in range(count):
            at = slice(q * piece, (q + 1) * piece)
            first = short(1, q * piece, piece, lanes)
            factor[at, lanes] = first
            kept[at, lanes] = skip[:, lanes] * kept[at, lanes] * first

    chunk = 32
    group = lane_group(chunk, width)
    sign = 1.0 - 2.0 * (lax.broadcasted_iota(jnp.int32, (chunk, LANES), 0) % 2).astype(jnp.float32)

    def read(ref, begin, tile):
        lanes = slice(tile * LANES, (tile + 1) * LANES)
        return (
            ref[pl.ds(pl.multiple_of(begin, chunk), chunk), lanes],
            ref[pl.ds(pl.multiple_of(rows + begin, chunk), chunk), lanes],
        )

    def shifted(blocks, tile, places):
        turned = pltpu.roll(blocks[tile], places * width, 1)
        before = pltpu.roll(blocks[tile - 1], places * width, 1) if tile > 0 else 0.0
        return jnp.where(group >= places, turned, before)

    filters(arrived)
    taps = jnp.concatenate(
        [
            jnp.concatenate(unpack(lambda i: recv_h[i, held], tile), axis=0)
            for held in range(filters_held)
            for tile in range(share_tiles)
        ],
        axis=1,
    ).astype(jnp.bfloat16)
    spec_h[...] = dot(table[0], taps) + dot(table[1], taps)
    for held in range(filters_held):

        def spread_chunk(index, carry):
            begin = index * chunk
            at = pl.ds(pl.multiple_of(begin, chunk), chunk)
            loaded = [
                read(spec_h, begin, held * share_tiles + tile) for tile in range(share_tiles)
            ]
            real = [pair[0] for pair in loaded]
            imag = [pair[1] for pair in loaded]
            for tile in range(share_tiles):
                both = (
                    real[tile] - sign * shifted(imag, tile, 1),
                    imag[tile] + sign * shifted(real, tile, 1),
                )
                for part, block in enumerate(both):
                    for k, wide in enumerate(spread_groups(block, width)):
                        spread[held, k, tile, part, at, :] = wide
            return carry

        lax.fori_loop(0, rows // chunk, spread_chunk, 0)

    for stage in range(shares):
        share, held = behind(stage), 0 if crossed else stage
        values(stage, arrived)
        block = jnp.concatenate(
            [
                jnp.concatenate(unpack(lambda i: recv_g[share, i], tile), axis=0)
                for tile in range(share_tiles)
            ],
            axis=1,
        )
        high, low = halves(block)
        both = dot(table[0], jnp.concatenate([high, low], axis=1))
        spec[...] = both[:, :wide] + both[:, wide:] + dot(table[1], high)

        def product_chunk(index, carry):
            begin = index * chunk
            at = pl.ds(pl.multiple_of(begin, chunk), chunk)
            also = pl.ds(pl.multiple_of(rows + begin, chunk), chunk)
            loaded = [read(spec, begin, tile) for tile in range(share_tiles)]
            real = [pair[0] for pair in loaded]
            imag = [pair[1] for pair in loaded]

            def step(k, sums):
                sums = list(sums)
                moved_real = [shifted(real, tile, k) for tile in range(share_tiles)]
                moved_imag = [shifted(imag, tile, k) for tile in range(share_tiles)]
                for apart in range(share_tiles):
                    kr = spread[held, k, apart, 0, at, :]
                    ki = spread[held, k, apart, 1, at, :]
                    for tile in range(apart, share_tiles):
                        xr, xi = moved_real[tile - apart], moved_imag[tile - apart]
                        sums[2 * tile] = sums[2 * tile] + (xr * kr - xi * ki)
                        sums[2 * tile + 1] = sums[2 * tile + 1] + (xr * ki + xi * kr)
                return tuple(sums)

            zero = jnp.zeros((chunk, LANES), jnp.float32)
            sums = loop(0, count, step, (zero,) * (2 * share_tiles))
            for tile in range(share_tiles):
                lanes = slice(tile * LANES, (tile + 1) * LANES)
                for where, total in ((at, sums[2 * tile]), (also, sums[2 * tile + 1])):
                    high, low = halves(total)
                    prod[where, lanes] = high
                    prod[where, slice(wide + lanes.start, wide + lanes.stop)] = low
            return carry

        lax.fori_loop(0, rows // chunk, product_chunk, 0)

        both = dot(back_table[0], prod[...])
        long_rows = both[:, :wide] + both[:, wide:] + dot(back_table[1], prod[:, :wide])
        for tile in range(share_tiles):
            lanes = slice(tile * LANES, (tile + 1) * LANES)
            parts = [long_rows[q * piece : (q + 1) * piece, lanes] for q in range(count)]
            for q, part in enumerate(exchange_groups(parts, width)):
                send_r[share, tile * count + q] = part
        results(stage, start)
        if stage == 0 or not crossed:
            recv_r[share, pl.ds(me, 1)] = send_r[share, pl.ds(me, 1)]

    leaving = []
    for stage in range(shares):
        share = ahead(stage)
        results(stage, arrived)
        for tile in range(share_tiles):
            lanes = lanes_of(share, tile)
            for q, part in enumerate(unpack(lambda i: recv_r[share, i], tile)):
                at = slice(q * piece, (q + 1) * piece)
                out[at, lanes] = (factor[at, lanes] * part + kept[at, lanes]).astype(out.dtype)
        lanes = pl.ds(pl.multiple_of(share * wide, LANES), wide)
        leaving.append(
            pltpu.make_async_copy(out.at[:, lanes], out_hbm.at[:, lanes], out_sem.at[stage])
        )
        leaving[-1].start()
    filters(left)
    for stage in range(shares):
        values(stage, left)
        results(stage, left)
    for copy in leaving:
        copy.wait()


def body(gate_stream, outer_stream, value_stream, short_weight, long_filter, skip_gain):
    devices, groups = lax.axis_size("ctx"), lax.axis_size("groups")
    rows, channels = gate_stream.shape
    tiles = channels // LANES
    shares = 2
    while shares > 1 and (tiles % shares or rows * channels // (devices * shares * LANES) < 16):
        shares -= 1
    crossed = shares == groups > 1
    held = 1 if crossed else shares
    width = channels // (devices * shares)
    count = LANES // width
    piece = rows // count
    share_tiles = tiles // shares
    table = transform_table(rows)
    filter_type = jnp.bfloat16 if piece % 16 == 0 else jnp.float32
    full = pltpu.VMEM((shares, devices, piece, LANES), jnp.float32)
    part = pltpu.VMEM((devices, held, piece, LANES), filter_type)
    many = pltpu.SemaphoreType.DMA((shares, devices))
    operands = (
        gate_stream, outer_stream, value_stream, short_weight, long_filter, skip_gain[None, :],
        jnp.asarray(split(table)), jnp.asarray(split(table.T / rows)),
    )
    return pl.pallas_call(
        functools.partial(kernel, devices, groups, shares, crossed),
        out_shape=jax.ShapeDtypeStruct((rows, channels), jnp.bfloat16),
        in_specs=[pl.BlockSpec(memory_space=pltpu.HBM)] * len(operands),
        out_specs=pl.BlockSpec(memory_space=pltpu.HBM),
        scratch_shapes=[
            *(pltpu.VMEM(each.shape, each.dtype) for each in operands),
            pltpu.VMEM((3, RIM + rows, channels), jnp.float32),
            pltpu.VMEM((3, 16, channels), jnp.bfloat16),
            part, part, full, full, full, full,
            pltpu.VMEM((2 * rows, share_tiles * LANES), jnp.float32),
            pltpu.VMEM((2 * rows, held * share_tiles * LANES), jnp.float32),
            pltpu.VMEM((held, count, share_tiles, 2, rows, LANES), jnp.float32),
            pltpu.VMEM((2 * rows, 2 * share_tiles * LANES), jnp.bfloat16),
            pltpu.VMEM((rows, channels), jnp.float32),
            pltpu.VMEM((rows, channels), jnp.float32),
            pltpu.VMEM((rows, channels), jnp.bfloat16),
            pltpu.SemaphoreType.DMA((len(operands),)),
            pltpu.SemaphoreType.DMA((shares,)),
            pltpu.SemaphoreType.DMA((3,)),
            pltpu.SemaphoreType.DMA((3,)),
            pltpu.SemaphoreType.DMA((devices,)),
            pltpu.SemaphoreType.DMA((devices,)),
            many, many, many, many,
        ],
        compiler_params=pltpu.CompilerParams(
            collective_id=0, has_side_effects=True, vmem_limit_bytes=64 * 1024 * 1024 - 320 * 1024
        ),
        cost_estimate=pl.CostEstimate(
            flops=2 * 16 * rows * rows * channels, bytes_accessed=4 * rows * channels, transcendentals=0
        ),
    )(*operands)


def solution(mesh):
    placed = (
        P(("groups", "ctx"), "ch"),
        P(("groups", "ctx"), "ch"),
        P(("groups", "ctx"), "ch"),
        P(None, None, "ch"),
        P("ctx", "ch"),
        P("ch"),
    )
    return jax.shard_map(
        body, mesh=mesh, in_specs=placed, out_specs=P(("groups", "ctx"), "ch"), check_vma=False
    )
```

```python
import functools

import jax
import jax.numpy as jnp
import numpy as np
from jax import lax
from jax.experimental import pallas as pl
from jax.experimental.pallas import tpu as pltpu
from jax.sharding import PartitionSpec as P

LANES = 128
RIM = 8


def loop(begin, end, step, carry):
    if end - begin <= 8:
        for i in range(begin, end):
            carry = step(i, carry)
        return carry
    return lax.fori_loop(begin, end, step, carry)


def transform_table(rows):
    freq = np.arange(rows)[:, None]
    time = np.arange(rows)[None, :]
    phase = ((2 * freq + 1) * time % (4 * rows)) * (np.pi / (2 * rows))
    return np.concatenate([np.cos(phase), -np.sin(phase)], axis=0)


def split(table):
    table = np.asarray(table, np.float32)
    high = table.astype(jnp.bfloat16)
    low = (table - high.astype(np.float32)).astype(jnp.bfloat16)
    return np.stack([high, low])


def halves(value):
    high = value.astype(jnp.bfloat16)
    low = (value - high.astype(jnp.float32)).astype(jnp.bfloat16)
    return high, low


def dot(a, b):
    return jnp.dot(a, b, preferred_element_type=jnp.float32)


def lane_group(rows, width):
    return lax.broadcasted_iota(jnp.int32, (rows, LANES), 1) // width


def exchange_groups(parts, width):
    parts = list(parts)
    count = LANES // width
    group = lane_group(parts[0].shape[0], width)
    span = 1
    while span < count:
        keep = (group & span) == 0
        for q in range(count):
            if q & span == 0:
                low, high = parts[q], parts[q | span]
                parts[q] = jnp.where(keep, low, pltpu.roll(high, span * width, 1))
                parts[q | span] = jnp.where(keep, pltpu.roll(low, LANES - span * width, 1), high)
        span *= 2
    return parts


def spread_groups(block, width):
    count = LANES // width
    group = lane_group(block.shape[0], width)
    result = [block]
    span = count // 2
    while span:
        keep = (group & span) == 0
        wider = []
        for each in result:
            turned = pltpu.roll(each, span * width, 1)
            wider += [jnp.where(keep, each, turned), jnp.where(keep, turned, each)]
        result = wider
        span //= 2
    return result


def kernel(
    devices, groups, shares, crossed, gate_hbm, outer_hbm, value_hbm, weight_hbm, filt_hbm, skip_hbm,
    table_hbm, back_hbm, out_hbm,
    gate, outer, value, weight, filt, skip, table, back_table,
    ext, rim, send_h, recv_h, send_g, recv_g, send_r, recv_r, spec, spec_h, spread, prod, kept, factor, out,
    load_sem, out_sem, rim_send, rim_recv, h_send, h_recv, g_send, g_recv, r_send, r_recv,
):
    rows, channels = gate.shape
    width = channels // (devices * shares)
    count = LANES // width
    piece = rows // count
    tiles = channels // LANES
    share_tiles = tiles // shares
    wide = share_tiles * LANES
    filters_held = 1 if crossed else shares
    me = lax.axis_index("ctx")
    mine = lax.axis_index("groups")

    def partner(distance):
        return lax.rem(me + distance, devices)

    def ahead(stage):
        return lax.rem(mine + stage, groups) if crossed else stage

    def behind(stage):
        return lax.rem(mine + groups - stage, groups) if crossed else stage

    def distances(stage):
        return 0 if crossed and stage > 0 else 1, devices

    def device_at(group, place):
        return {"groups": group if crossed else mine, "ctx": place}

    barrier = pltpu.get_barrier_semaphore()
    met = 0
    for stage in range(shares if crossed else 1):

        def greet(distance, carry):
            pl.semaphore_signal(
                barrier, inc=1, device_id=device_at(ahead(stage), partner(distance)),
                device_id_type=pl.DeviceIdType.MESH,
            )
            return carry

        loop(*distances(stage), greet, 0)
        met += devices - distances(stage)[0]

    pairs = (
        (filt_hbm, filt), (gate_hbm, gate), (value_hbm, value), (weight_hbm, weight),
        (outer_hbm, outer), (skip_hbm, skip), (table_hbm, table), (back_hbm, back_table),
    )
    loads = [pltpu.make_async_copy(src, dst, load_sem.at[i]) for i, (src, dst) in enumerate(pairs)]
    for load in loads:
        load.start()

    def lanes_of(share, tile):
        begin = (share * share_tiles + tile) * LANES
        return pl.ds(pl.multiple_of(begin, LANES), LANES)

    def pack(source, share, store):
        for tile in range(share_tiles):
            lanes = lanes_of(share, tile)
            parts = [source(q * piece, piece, lanes) for q in range(count)]
            for q, part in enumerate(exchange_groups(parts, width)):
                store(tile * count + q, part)

    def unpack(read, tile):
        parts = [read(tile * count + q).astype(jnp.float32) for q in range(count)]
        return exchange_groups(parts, width)

    def exchange(span, group, sent, landed, send_sem, recv_sem, act):
        def step(distance, carry):
            copy = pltpu.make_async_remote_copy(
                src_ref=sent(partner(distance)),
                dst_ref=landed,
                send_sem=send_sem.at[distance],
                recv_sem=recv_sem.at[distance],
                device_id=device_at(group, partner(distance)),
                device_id_type=pl.DeviceIdType.MESH,
            )
            act(copy)
            return carry

        loop(*span, step, 0)

    def filters(act):
        exchange(
            (1, devices), mine, lambda i: send_h.at[i], recv_h.at[me], h_send, h_recv, act
        )

    def values(stage, act):
        exchange(
            distances(stage), ahead(stage), lambda i: send_g.at[ahead(stage), i],
            recv_g.at[mine if crossed else stage, me], g_send.at[stage], g_recv.at[stage], act,
        )

    def results(stage, act):
        exchange(
            distances(stage), behind(stage), lambda i: send_r.at[behind(stage), i],
            recv_r.at[mine if crossed else stage, me], r_send.at[stage], r_recv.at[stage], act,
        )

    def start(copy):
        copy.start()

    def arrived(copy):
        copy.wait_recv()

    def left(copy):
        copy.wait_send()

    pl.semaphore_wait(barrier, met)
    rim_copies = [
        pltpu.make_async_remote_copy(
            src_ref=stream.at[rows - rim.shape[1] :],
            dst_ref=rim.at[i],
            send_sem=rim_send.at[i],
            recv_sem=rim_recv.at[i],
            device_id={"groups": mine, "ctx": partner(1)},
            device_id_type=pl.DeviceIdType.MESH,
        )
        for i, stream in enumerate((gate_hbm, outer_hbm, value_hbm))
    ]
    for i in (0, 2, 1):
        rim_copies[i].start()

    loads[0].wait()
    for held in range(filters_held):

        def store_filter(device, part):
            send_h[device, held] = part.astype(send_h.dtype)

        pack(
            lambda r, n, lanes: filt[r : r + n, lanes].astype(jnp.float32),
            mine if crossed else held, store_filter,
        )
    filters(start)

    def short(i, r, n, lanes):
        taps = weight[i, :, lanes].astype(jnp.float32)
        total = None
        for offset in range(taps.shape[0]):
            begin = r + RIM - offset
            term = taps[offset : offset + 1] * ext[i, begin : begin + n, lanes]
            total = term if total is None else total + term
        return total

    def gated(r, n, lanes):
        result = short(0, r, n, lanes) * short(2, r, n, lanes)
        kept[r : r + n, lanes] = result
        return result

    ext[:, :RIM, :] = jnp.zeros((3, RIM, channels), jnp.float32)
    for load in loads[1:4]:
        load.wait()
    ext[0, RIM:, :] = gate[...].astype(jnp.float32)
    ext[2, RIM:, :] = value[...].astype(jnp.float32)
    for stage in range(shares):

        def store_value(device, part):
            send_g[ahead(stage), device] = part

        pack(gated, ahead(stage), store_value)
    for i in (0, 2):
        rim_copies[i].wait()
        last = rim[i].astype(jnp.float32)[rim.shape[1] - RIM :]
        ext[i, :RIM, :] = jnp.where(me > 0, last, 0.0)
    first_lanes = lane_group(RIM, width) == 0
    for stage in range(shares):
        share = ahead(stage)
        for tile in range(share_tiles):
            block = gated(0, RIM, lanes_of(share, tile))
            for q in range(count):
                device = tile * count + q
                moved = pltpu.roll(block, (LANES - q * width) % LANES, 1)
                send_g[share, device, :RIM] = jnp.where(
                    first_lanes, moved, send_g[share, device, :RIM]
                )
        if stage == 0:
            values(stage, start)
    for stage in range(1 if crossed else shares):
        recv_g[behind(stage), pl.ds(me, 1)] = send_g[ahead(stage), pl.ds(me, 1)]
    recv_h[pl.ds(me, 1)] = send_h[pl.ds(me, 1)]
    for load in loads[4:]:
        load.wait()

    rim_copies[1].wait()
    ext[1, :RIM, :] = jnp.where(me > 0, rim[1].astype(jnp.float32)[rim.shape[1] - RIM :], 0.0)
    ext[1, RIM:, :] = outer[...].astype(jnp.float32)
    for tile in range(tiles):
        lanes = slice(tile * LANES, (tile + 1) * LANES)
        for q in range(count):
            at = slice(q * piece, (q + 1) * piece)
            first = short(1, q * piece, piece, lanes)
            factor[at, lanes] = first
            kept[at, lanes] = skip[:, lanes] * kept[at, lanes] * first

    chunk = 32
    group = lane_group(chunk, width)
    sign = 1.0 - 2.0 * (lax.broadcasted_iota(jnp.int32, (chunk, LANES), 0) % 2).astype(jnp.float32)

    def read(ref, begin, tile):
        lanes = slice(tile * LANES, (tile + 1) * LANES)
        return (
            ref[pl.ds(pl.multiple_of(begin, chunk), chunk), lanes],
            ref[pl.ds(pl.multiple_of(rows + begin, chunk), chunk), lanes],
        )

    def shifted(blocks, tile, places):
        turned = pltpu.roll(blocks[tile], places * width, 1)
        before = pltpu.roll(blocks[tile - 1], places * width, 1) if tile > 0 else 0.0
        return jnp.where(group >= places, turned, before)

    for stage in range(1, shares):
        values(stage - 1, left)
        values(stage, start)

    filters(arrived)
    taps = jnp.concatenate(
        [
            jnp.concatenate(unpack(lambda i: recv_h[i, held], tile), axis=0)
            for held in range(filters_held)
            for tile in range(share_tiles)
        ],
        axis=1,
    ).astype(jnp.bfloat16)
    spec_h[...] = dot(table[0], taps) + dot(table[1], taps)
    for held in range(filters_held):

        def spread_chunk(index, carry):
            begin = index * chunk
            at = pl.ds(pl.multiple_of(begin, chunk), chunk)
            loaded = [
                read(spec_h, begin, held * share_tiles + tile) for tile in range(share_tiles)
            ]
            real = [pair[0] for pair in loaded]
            imag = [pair[1] for pair in loaded]
            for tile in range(share_tiles):
                both = (
                    real[tile] - sign * shifted(imag, tile, 1),
                    imag[tile] + sign * shifted(real, tile, 1),
                )
                for part, block in enumerate(both):
                    for k, wide in enumerate(spread_groups(block, width)):
                        spread[held, k, tile, part, at, :] = wide
            return carry

        lax.fori_loop(0, rows // chunk, spread_chunk, 0)

    for stage in range(shares):
        share, held = behind(stage), 0 if crossed else stage
        values(stage, arrived)
        block = jnp.concatenate(
            [
                jnp.concatenate(unpack(lambda i: recv_g[share, i], tile), axis=0)
                for tile in range(share_tiles)
            ],
            axis=1,
        )
        high, low = halves(block)
        both = dot(table[0], jnp.concatenate([high, low], axis=1))
        spec[...] = both[:, :wide] + both[:, wide:] + dot(table[1], high)

        def product_chunk(index, carry):
            begin = index * chunk
            at = pl.ds(pl.multiple_of(begin, chunk), chunk)
            also = pl.ds(pl.multiple_of(rows + begin, chunk), chunk)
            loaded = [read(spec, begin, tile) for tile in range(share_tiles)]
            real = [pair[0] for pair in loaded]
            imag = [pair[1] for pair in loaded]

            def step(k, sums):
                sums = list(sums)
                moved_real = [shifted(real, tile, k) for tile in range(share_tiles)]
                moved_imag = [shifted(imag, tile, k) for tile in range(share_tiles)]
                for apart in range(share_tiles):
                    kr = spread[held, k, apart, 0, at, :]
                    ki = spread[held, k, apart, 1, at, :]
                    for tile in range(apart, share_tiles):
                        xr, xi = moved_real[tile - apart], moved_imag[tile - apart]
                        sums[2 * tile] = sums[2 * tile] + (xr * kr - xi * ki)
                        sums[2 * tile + 1] = sums[2 * tile + 1] + (xr * ki + xi * kr)
                return tuple(sums)

            zero = jnp.zeros((chunk, LANES), jnp.float32)
            sums = loop(0, count, step, (zero,) * (2 * share_tiles))
            for tile in range(share_tiles):
                lanes = slice(tile * LANES, (tile + 1) * LANES)
                for where, total in ((at, sums[2 * tile]), (also, sums[2 * tile + 1])):
                    high, low = halves(total)
                    prod[where, lanes] = high
                    prod[where, slice(wide + lanes.start, wide + lanes.stop)] = low
            return carry

        lax.fori_loop(0, rows // chunk, product_chunk, 0)

        both = dot(back_table[0], prod[...])
        long_rows = both[:, :wide] + both[:, wide:] + dot(back_table[1], prod[:, :wide])
        for tile in range(share_tiles):
            lanes = slice(tile * LANES, (tile + 1) * LANES)
            parts = [long_rows[q * piece : (q + 1) * piece, lanes] for q in range(count)]
            for q, part in enumerate(exchange_groups(parts, width)):
                send_r[share, tile * count + q] = part
        results(stage, start)
        if stage == 0 or not crossed:
            recv_r[share, pl.ds(me, 1)] = send_r[share, pl.ds(me, 1)]

    leaving = []
    for stage in range(shares):
        share = ahead(stage)
        results(stage, arrived)
        for tile in range(share_tiles):
            lanes = lanes_of(share, tile)
            for q, part in enumerate(unpack(lambda i: recv_r[share, i], tile)):
                at = slice(q * piece, (q + 1) * piece)
                out[at, lanes] = (factor[at, lanes] * part + kept[at, lanes]).astype(out.dtype)
        lanes = pl.ds(pl.multiple_of(share * wide, LANES), wide)
        leaving.append(
            pltpu.make_async_copy(out.at[:, lanes], out_hbm.at[:, lanes], out_sem.at[stage])
        )
        leaving[-1].start()
    filters(left)
    values(shares - 1, left)
    for stage in range(shares):
        results(stage, left)
    for copy in leaving:
        copy.wait()


def body(gate_stream, outer_stream, value_stream, short_weight, long_filter, skip_gain):
    devices, groups = lax.axis_size("ctx"), lax.axis_size("groups")
    rows, channels = gate_stream.shape
    tiles = channels // LANES
    shares = 2
    while shares > 1 and (tiles % shares or rows * channels // (devices * shares * LANES) < 16):
        shares -= 1
    crossed = shares == groups > 1
    held = 1 if crossed else shares
    width = channels // (devices * shares)
    count = LANES // width
    piece = rows // count
    share_tiles = tiles // shares
    table = transform_table(rows)
    filter_type = jnp.bfloat16 if piece % 16 == 0 else jnp.float32
    full = pltpu.VMEM((shares, devices, piece, LANES), jnp.float32)
    part = pltpu.VMEM((devices, held, piece, LANES), filter_type)
    many = pltpu.SemaphoreType.DMA((shares, devices))
    operands = (
        gate_stream, outer_stream, value_stream, short_weight, long_filter, skip_gain[None, :],
        jnp.asarray(split(table)), jnp.asarray(split(table.T / rows)),
    )
    return pl.pallas_call(
        functools.partial(kernel, devices, groups, shares, crossed),
        out_shape=jax.ShapeDtypeStruct((rows, channels), jnp.bfloat16),
        in_specs=[pl.BlockSpec(memory_space=pltpu.HBM)] * len(operands),
        out_specs=pl.BlockSpec(memory_space=pltpu.HBM),
        scratch_shapes=[
            *(pltpu.VMEM(each.shape, each.dtype) for each in operands),
            pltpu.VMEM((3, RIM + rows, channels), jnp.float32),
            pltpu.VMEM((3, 16, channels), jnp.bfloat16),
            part, part, full, full, full, full,
            pltpu.VMEM((2 * rows, share_tiles * LANES), jnp.float32),
            pltpu.VMEM((2 * rows, held * share_tiles * LANES), jnp.float32),
            pltpu.VMEM((held, count, share_tiles, 2, rows, LANES), jnp.float32),
            pltpu.VMEM((2 * rows, 2 * share_tiles * LANES), jnp.bfloat16),
            pltpu.VMEM((rows, channels), jnp.float32),
            pltpu.VMEM((rows, channels), jnp.float32),
            pltpu.VMEM((rows, channels), jnp.bfloat16),
            pltpu.SemaphoreType.DMA((len(operands),)),
            pltpu.SemaphoreType.DMA((shares,)),
            pltpu.SemaphoreType.DMA((3,)),
            pltpu.SemaphoreType.DMA((3,)),
            pltpu.SemaphoreType.DMA((devices,)),
            pltpu.SemaphoreType.DMA((devices,)),
            many, many, many, many,
        ],
        compiler_params=pltpu.CompilerParams(
            collective_id=0, has_side_effects=True, vmem_limit_bytes=64 * 1024 * 1024 - 320 * 1024
        ),
        cost_estimate=pl.CostEstimate(
            flops=2 * 16 * rows * rows * channels, bytes_accessed=4 * rows * channels, transcendentals=0
        ),
    )(*operands)


def solution(mesh):
    placed = (
        P(("groups", "ctx"), "ch"),
        P(("groups", "ctx"), "ch"),
        P(("groups", "ctx"), "ch"),
        P(None, None, "ch"),
        P("ctx", "ch"),
        P("ch"),
    )
    return jax.shard_map(
        body, mesh=mesh, in_specs=placed, out_specs=P(("groups", "ctx"), "ch"), check_vma=False
    )
```

```python
import functools

import jax
import jax.numpy as jnp
import numpy as np
from jax import lax
from jax.experimental import pallas as pl
from jax.experimental.pallas import tpu as pltpu
from jax.sharding import PartitionSpec as P

LANES = 128
RIM = 8


def loop(begin, end, step, carry):
    if end - begin <= 8:
        for i in range(begin, end):
            carry = step(i, carry)
        return carry
    return lax.fori_loop(begin, end, step, carry)


def transform_table(rows):
    freq = np.arange(rows)[:, None]
    time = np.arange(rows)[None, :]
    phase = ((2 * freq + 1) * time % (4 * rows)) * (np.pi / (2 * rows))
    return np.concatenate([np.cos(phase), -np.sin(phase)], axis=0)


def split(table):
    table = np.asarray(table, np.float32)
    high = table.astype(jnp.bfloat16)
    low = (table - high.astype(np.float32)).astype(jnp.bfloat16)
    return np.stack([high, low])


def halves(value):
    high = value.astype(jnp.bfloat16)
    low = (value - high.astype(jnp.float32)).astype(jnp.bfloat16)
    return high, low


def dot(a, b):
    return jnp.dot(a, b, preferred_element_type=jnp.float32)


def lane_group(rows, width):
    return lax.broadcasted_iota(jnp.int32, (rows, LANES), 1) // width


def exchange_groups(parts, width):
    parts = list(parts)
    count = LANES // width
    group = lane_group(parts[0].shape[0], width)
    span = 1
    while span < count:
        keep = (group & span) == 0
        for q in range(count):
            if q & span == 0:
                low, high = parts[q], parts[q | span]
                parts[q] = jnp.where(keep, low, pltpu.roll(high, span * width, 1))
                parts[q | span] = jnp.where(keep, pltpu.roll(low, LANES - span * width, 1), high)
        span *= 2
    return parts


def spread_groups(block, width):
    count = LANES // width
    group = lane_group(block.shape[0], width)
    result = [block]
    span = count // 2
    while span:
        keep = (group & span) == 0
        wider = []
        for each in result:
            turned = pltpu.roll(each, span * width, 1)
            wider += [jnp.where(keep, each, turned), jnp.where(keep, turned, each)]
        result = wider
        span //= 2
    return result


def kernel(
    devices, groups, shares, crossed, gate_hbm, outer_hbm, value_hbm, weight_hbm, filt_hbm, skip_hbm,
    table_hbm, back_hbm, out_hbm,
    gate, outer, value, weight, filt, skip, table, back_table,
    ext, rim, send_h, recv_h, send_g, recv_g, send_r, recv_r, spec, spec_h, spread, prod, kept, factor, out,
    load_sem, out_sem, rim_send, rim_recv, h_send, h_recv, g_send, g_recv, r_send, r_recv,
):
    rows, channels = gate.shape
    width = channels // (devices * shares)
    count = LANES // width
    piece = rows // count
    tiles = channels // LANES
    share_tiles = tiles // shares
    wide = share_tiles * LANES
    filters_held = 1 if crossed else shares
    me = lax.axis_index("ctx")
    mine = lax.axis_index("groups")

    def partner(distance):
        return lax.rem(me + distance, devices)

    def ahead(stage):
        return lax.rem(mine + stage, groups) if crossed else stage

    def behind(stage):
        return lax.rem(mine + groups - stage, groups) if crossed else stage

    def distances(stage):
        return 0 if crossed and stage > 0 else 1, devices

    def device_at(group, place):
        return {"groups": group if crossed else mine, "ctx": place}

    barrier = pltpu.get_barrier_semaphore()
    met = 0
    for stage in range(shares if crossed else 1):

        def greet(distance, carry):
            pl.semaphore_signal(
                barrier, inc=1, device_id=device_at(ahead(stage), partner(distance)),
                device_id_type=pl.DeviceIdType.MESH,
            )
            return carry

        loop(*distances(stage), greet, 0)
        met += devices - distances(stage)[0]

    pairs = (
        (filt_hbm, filt), (gate_hbm, gate), (value_hbm, value), (weight_hbm, weight),
        (outer_hbm, outer), (skip_hbm, skip), (table_hbm, table), (back_hbm, back_table),
    )
    loads = [pltpu.make_async_copy(src, dst, load_sem.at[i]) for i, (src, dst) in enumerate(pairs)]
    for load in loads:
        load.start()

    def lanes_of(share, tile):
        begin = (share * share_tiles + tile) * LANES
        return pl.ds(pl.multiple_of(begin, LANES), LANES)

    def pack(source, share, store):
        for tile in range(share_tiles):
            lanes = lanes_of(share, tile)
            parts = [source(q * piece, piece, lanes) for q in range(count)]
            for q, part in enumerate(exchange_groups(parts, width)):
                store(tile * count + q, part)

    def unpack(read, tile):
        parts = [read(tile * count + q).astype(jnp.float32) for q in range(count)]
        return exchange_groups(parts, width)

    def exchange(span, group, sent, landed, send_sem, recv_sem, act):
        def step(distance, carry):
            copy = pltpu.make_async_remote_copy(
                src_ref=sent(partner(distance)),
                dst_ref=landed,
                send_sem=send_sem.at[distance],
                recv_sem=recv_sem.at[distance],
                device_id=device_at(group, partner(distance)),
                device_id_type=pl.DeviceIdType.MESH,
            )
            act(copy)
            return carry

        loop(*span, step, 0)

    def filters(act):
        exchange(
            (1, devices), mine, lambda i: send_h.at[i], recv_h.at[me], h_send, h_recv, act
        )

    def values(stage, act):
        exchange(
            distances(stage), ahead(stage), lambda i: send_g.at[ahead(stage), i],
            recv_g.at[mine if crossed else stage, me], g_send.at[stage], g_recv.at[stage], act,
        )

    def results(stage, act):
        exchange(
            distances(stage), behind(stage), lambda i: send_r.at[behind(stage), i],
            recv_r.at[mine if crossed else stage, me], r_send.at[stage], r_recv.at[stage], act,
        )

    def start(copy):
        copy.start()

    def arrived(copy):
        copy.wait_recv()

    def left(copy):
        copy.wait_send()

    pl.semaphore_wait(barrier, met)
    rim_copies = [
        pltpu.make_async_remote_copy(
            src_ref=stream.at[rows - rim.shape[1] :],
            dst_ref=rim.at[i],
            send_sem=rim_send.at[i],
            recv_sem=rim_recv.at[i],
            device_id={"groups": mine, "ctx": partner(1)},
            device_id_type=pl.DeviceIdType.MESH,
        )
        for i, stream in enumerate((gate_hbm, outer_hbm, value_hbm))
    ]
    for i in (0, 2, 1):
        rim_copies[i].start()

    loads[0].wait()
    for held in range(filters_held):

        def store_filter(device, part):
            send_h[device, held] = part.astype(send_h.dtype)

        pack(
            lambda r, n, lanes: filt[r : r + n, lanes].astype(jnp.float32),
            mine if crossed else held, store_filter,
        )
    filters(start)

    def short(i, r, n, lanes):
        taps = weight[i, :, lanes].astype(jnp.float32)
        total = None
        for offset in range(taps.shape[0]):
            begin = r + RIM - offset
            term = taps[offset : offset + 1] * ext[i, begin : begin + n, lanes]
            total = term if total is None else total + term
        return total

    def gated(r, n, lanes):
        result = short(0, r, n, lanes) * short(2, r, n, lanes)
        kept[r : r + n, lanes] = result
        return result

    ext[:, :RIM, :] = jnp.zeros((3, RIM, channels), jnp.float32)
    for load in loads[1:4]:
        load.wait()
    ext[0, RIM:, :] = gate[...].astype(jnp.float32)
    ext[2, RIM:, :] = value[...].astype(jnp.float32)
    for stage in range(shares):

        def store_value(device, part):
            send_g[ahead(stage), device] = part

        pack(gated, ahead(stage), store_value)
    for i in (0, 2):
        rim_copies[i].wait()
        last = rim[i].astype(jnp.float32)[rim.shape[1] - RIM :]
        ext[i, :RIM, :] = jnp.where(me > 0, last, 0.0)
    first_lanes = lane_group(RIM, width) == 0
    for stage in range(shares):
        share = ahead(stage)
        for tile in range(share_tiles):
            block = gated(0, RIM, lanes_of(share, tile))
            for q in range(count):
                device = tile * count + q
                moved = pltpu.roll(block, (LANES - q * width) % LANES, 1)
                send_g[share, device, :RIM] = jnp.where(
                    first_lanes, moved, send_g[share, device, :RIM]
                )
        values(stage, start)
    for stage in range(1 if crossed else shares):
        recv_g[behind(stage), pl.ds(me, 1)] = send_g[ahead(stage), pl.ds(me, 1)]
    recv_h[pl.ds(me, 1)] = send_h[pl.ds(me, 1)]
    for load in loads[4:]:
        load.wait()

    rim_copies[1].wait()
    ext[1, :RIM, :] = jnp.where(me > 0, rim[1].astype(jnp.float32)[rim.shape[1] - RIM :], 0.0)
    ext[1, RIM:, :] = outer[...].astype(jnp.float32)
    for tile in range(tiles):
        lanes = slice(tile * LANES, (tile + 1) * LANES)
        for q in range(count):
            at = slice(q * piece, (q + 1) * piece)
            first = short(1, q * piece, piece, lanes)
            factor[at, lanes] = first
            kept[at, lanes] = skip[:, lanes] * kept[at, lanes] * first

    chunk = 32
    group = lane_group(chunk, width)
    sign = 1.0 - 2.0 * (lax.broadcasted_iota(jnp.int32, (chunk, LANES), 0) % 2).astype(jnp.float32)

    def rows_at(begin):
        if isinstance(begin, int):
            return slice(begin, begin + chunk)
        return pl.ds(pl.multiple_of(begin, chunk), chunk)

    def read(ref, begin, tile):
        lanes = slice(tile * LANES, (tile + 1) * LANES)
        return (
            ref[rows_at(begin), lanes],
            ref[rows_at(rows + begin), lanes],
        )

    def shifted(blocks, tile, places):
        turned = pltpu.roll(blocks[tile], places * width, 1)
        before = pltpu.roll(blocks[tile - 1], places * width, 1) if tile > 0 else 0.0
        return jnp.where(group >= places, turned, before)

    filters(arrived)
    taps = jnp.concatenate(
        [
            jnp.concatenate(unpack(lambda i: recv_h[i, held], tile), axis=0)
            for held in range(filters_held)
            for tile in range(share_tiles)
        ],
        axis=1,
    ).astype(jnp.bfloat16)
    spec_h[...] = dot(table[0], taps) + dot(table[1], taps)
    for held in range(filters_held):

        def spread_chunk(index, carry):
            begin = index * chunk
            at = rows_at(begin)
            loaded = [
                read(spec_h, begin, held * share_tiles + tile) for tile in range(share_tiles)
            ]
            real = [pair[0] for pair in loaded]
            imag = [pair[1] for pair in loaded]
            for tile in range(share_tiles):
                both = (
                    real[tile] - sign * shifted(imag, tile, 1),
                    imag[tile] + sign * shifted(real, tile, 1),
                )
                for part, block in enumerate(both):
                    for k, wide in enumerate(spread_groups(block, width)):
                        spread[held, k, tile, part, at, :] = wide
            return carry

        loop(0, rows // chunk, spread_chunk, 0)

    for stage in range(shares):
        share, held = behind(stage), 0 if crossed else stage
        values(stage, arrived)
        block = jnp.concatenate(
            [
                jnp.concatenate(unpack(lambda i: recv_g[share, i], tile), axis=0)
                for tile in range(share_tiles)
            ],
            axis=1,
        )
        high, low = halves(block)
        both = dot(table[0], jnp.concatenate([high, low], axis=1))
        spec[...] = both[:, :wide] + both[:, wide:] + dot(table[1], high)

        def product_chunk(index, carry):
            begin = index * chunk
            at = rows_at(begin)
            also = rows_at(rows + begin)
            loaded = [read(spec, begin, tile) for tile in range(share_tiles)]
            real = [pair[0] for pair in loaded]
            imag = [pair[1] for pair in loaded]

            def step(k, sums):
                sums = list(sums)
                moved_real = [shifted(real, tile, k) for tile in range(share_tiles)]
                moved_imag = [shifted(imag, tile, k) for tile in range(share_tiles)]
                for apart in range(share_tiles):
                    kr = spread[held, k, apart, 0, at, :]
                    ki = spread[held, k, apart, 1, at, :]
                    for tile in range(apart, share_tiles):
                        xr, xi = moved_real[tile - apart], moved_imag[tile - apart]
                        sums[2 * tile] = sums[2 * tile] + (xr * kr - xi * ki)
                        sums[2 * tile + 1] = sums[2 * tile + 1] + (xr * ki + xi * kr)
                return tuple(sums)

            zero = jnp.zeros((chunk, LANES), jnp.float32)
            sums = loop(0, count, step, (zero,) * (2 * share_tiles))
            for tile in range(share_tiles):
                lanes = slice(tile * LANES, (tile + 1) * LANES)
                for where, total in ((at, sums[2 * tile]), (also, sums[2 * tile + 1])):
                    high, low = halves(total)
                    prod[where, lanes] = high
                    prod[where, slice(wide + lanes.start, wide + lanes.stop)] = low
            return carry

        loop(0, rows // chunk, product_chunk, 0)

        both = dot(back_table[0], prod[...])
        long_rows = both[:, :wide] + both[:, wide:] + dot(back_table[1], prod[:, :wide])
        for tile in range(share_tiles):
            lanes = slice(tile * LANES, (tile + 1) * LANES)
            parts = [long_rows[q * piece : (q + 1) * piece, lanes] for q in range(count)]
            for q, part in enumerate(exchange_groups(parts, width)):
                send_r[share, tile * count + q] = part
        results(stage, start)
        if stage == 0 or not crossed:
            recv_r[share, pl.ds(me, 1)] = send_r[share, pl.ds(me, 1)]

    leaving = []
    for stage in range(shares):
        share = ahead(stage)
        results(stage, arrived)
        for tile in range(share_tiles):
            lanes = lanes_of(share, tile)
            for q, part in enumerate(unpack(lambda i: recv_r[share, i], tile)):
                at = slice(q * piece, (q + 1) * piece)
                out[at, lanes] = (factor[at, lanes] * part + kept[at, lanes]).astype(out.dtype)
        lanes = pl.ds(pl.multiple_of(share * wide, LANES), wide)
        leaving.append(
            pltpu.make_async_copy(out.at[:, lanes], out_hbm.at[:, lanes], out_sem.at[stage])
        )
        leaving[-1].start()
    filters(left)
    for stage in range(shares):
        values(stage, left)
        results(stage, left)
    for copy in leaving:
        copy.wait()


def body(gate_stream, outer_stream, value_stream, short_weight, long_filter, skip_gain):
    devices, groups = lax.axis_size("ctx"), lax.axis_size("groups")
    rows, channels = gate_stream.shape
    tiles = channels // LANES
    shares = 2
    while shares > 1 and (tiles % shares or rows * channels // (devices * shares * LANES) < 16):
        shares -= 1
    crossed = shares == groups > 1
    held = 1 if crossed else shares
    width = channels // (devices * shares)
    count = LANES // width
    piece = rows // count
    share_tiles = tiles // shares
    table = transform_table(rows)
    filter_type = jnp.bfloat16 if piece % 16 == 0 else jnp.float32
    full = pltpu.VMEM((shares, devices, piece, LANES), jnp.float32)
    part = pltpu.VMEM((devices, held, piece, LANES), filter_type)
    many = pltpu.SemaphoreType.DMA((shares, devices))
    operands = (
        gate_stream, outer_stream, value_stream, short_weight, long_filter, skip_gain[None, :],
        jnp.asarray(split(table)), jnp.asarray(split(table.T / rows)),
    )
    return pl.pallas_call(
        functools.partial(kernel, devices, groups, shares, crossed),
        out_shape=jax.ShapeDtypeStruct((rows, channels), jnp.bfloat16),
        in_specs=[pl.BlockSpec(memory_space=pltpu.HBM)] * len(operands),
        out_specs=pl.BlockSpec(memory_space=pltpu.HBM),
        scratch_shapes=[
            *(pltpu.VMEM(each.shape, each.dtype) for each in operands),
            pltpu.VMEM((3, RIM + rows, channels), jnp.float32),
            pltpu.VMEM((3, 16, channels), jnp.bfloat16),
            part, part, full, full, full, full,
            pltpu.VMEM((2 * rows, share_tiles * LANES), jnp.float32),
            pltpu.VMEM((2 * rows, held * share_tiles * LANES), jnp.float32),
            pltpu.VMEM((held, count, share_tiles, 2, rows, LANES), jnp.float32),
            pltpu.VMEM((2 * rows, 2 * share_tiles * LANES), jnp.bfloat16),
            pltpu.VMEM((rows, channels), jnp.float32),
            pltpu.VMEM((rows, channels), jnp.float32),
            pltpu.VMEM((rows, channels), jnp.bfloat16),
            pltpu.SemaphoreType.DMA((len(operands),)),
            pltpu.SemaphoreType.DMA((shares,)),
            pltpu.SemaphoreType.DMA((3,)),
            pltpu.SemaphoreType.DMA((3,)),
            pltpu.SemaphoreType.DMA((devices,)),
            pltpu.SemaphoreType.DMA((devices,)),
            many, many, many, many,
        ],
        compiler_params=pltpu.CompilerParams(
            collective_id=0, has_side_effects=True, vmem_limit_bytes=64 * 1024 * 1024 - 320 * 1024
        ),
        cost_estimate=pl.CostEstimate(
            flops=2 * 16 * rows * rows * channels, bytes_accessed=4 * rows * channels, transcendentals=0
        ),
    )(*operands)


def solution(mesh):
    placed = (
        P(("groups", "ctx"), "ch"),
        P(("groups", "ctx"), "ch"),
        P(("groups", "ctx"), "ch"),
        P(None, None, "ch"),
        P("ctx", "ch"),
        P("ch"),
    )
    return jax.shard_map(
        body, mesh=mesh, in_specs=placed, out_specs=P(("groups", "ctx"), "ch"), check_vma=False
    )
```

```python
import functools

import jax
import jax.numpy as jnp
import numpy as np
from jax import lax
from jax.experimental import pallas as pl
from jax.experimental.pallas import tpu as pltpu
from jax.sharding import PartitionSpec as P

LANES = 128
RIM = 8


def loop(begin, end, step, carry):
    if end - begin <= 8:
        for i in range(begin, end):
            carry = step(i, carry)
        return carry
    return lax.fori_loop(begin, end, step, carry)


def transform_table(rows):
    freq = np.arange(rows)[:, None]
    time = np.arange(rows)[None, :]
    phase = ((2 * freq + 1) * time % (4 * rows)) * (np.pi / (2 * rows))
    return np.concatenate([np.cos(phase), -np.sin(phase)], axis=0)


def split(table):
    table = np.asarray(table, np.float32)
    high = table.astype(jnp.bfloat16)
    low = (table - high.astype(np.float32)).astype(jnp.bfloat16)
    return np.stack([high, low])


def halves(value):
    high = value.astype(jnp.bfloat16)
    low = (value - high.astype(jnp.float32)).astype(jnp.bfloat16)
    return high, low


def dot(a, b):
    return jnp.dot(a, b, preferred_element_type=jnp.float32)


def lane_group(rows, width):
    return lax.broadcasted_iota(jnp.int32, (rows, LANES), 1) // width


def exchange_groups(parts, width):
    parts = list(parts)
    count = LANES // width
    group = lane_group(parts[0].shape[0], width)
    span = 1
    while span < count:
        keep = (group & span) == 0
        for q in range(count):
            if q & span == 0:
                low, high = parts[q], parts[q | span]
                parts[q] = jnp.where(keep, low, pltpu.roll(high, span * width, 1))
                parts[q | span] = jnp.where(keep, pltpu.roll(low, LANES - span * width, 1), high)
        span *= 2
    return parts


def spread_groups(block, width):
    count = LANES // width
    group = lane_group(block.shape[0], width)
    result = [block]
    span = count // 2
    while span:
        keep = (group & span) == 0
        wider = []
        for each in result:
            turned = pltpu.roll(each, span * width, 1)
            wider += [jnp.where(keep, each, turned), jnp.where(keep, turned, each)]
        result = wider
        span //= 2
    return result


def kernel(
    devices, groups, shares, crossed, gate_hbm, outer_hbm, value_hbm, weight_hbm, filt_hbm, skip_hbm,
    table_hbm, back_hbm, out,
    gate, outer, value, weight, filt, skip, table, back_table,
    ext, rim, send_h, recv_h, send_g, recv_g, send_r, recv_r, spec, spec_h, spread, prod, kept, factor,
    load_sem, rim_send, rim_recv, h_send, h_recv, g_send, g_recv, r_send, r_recv,
):
    rows, channels = gate.shape
    width = channels // (devices * shares)
    count = LANES // width
    piece = rows // count
    tiles = channels // LANES
    share_tiles = tiles // shares
    wide = share_tiles * LANES
    filters_held = 1 if crossed else shares
    me = lax.axis_index("ctx")
    mine = lax.axis_index("groups")

    def partner(distance):
        return lax.rem(me + distance, devices)

    def ahead(stage):
        return lax.rem(mine + stage, groups) if crossed else stage

    def behind(stage):
        return lax.rem(mine + groups - stage, groups) if crossed else stage

    def distances(stage):
        return 0 if crossed and stage > 0 else 1, devices

    def device_at(group, place):
        return {"groups": group if crossed else mine, "ctx": place}

    barrier = pltpu.get_barrier_semaphore()
    met = 0
    for stage in range(shares if crossed else 1):

        def greet(distance, carry):
            pl.semaphore_signal(
                barrier, inc=1, device_id=device_at(ahead(stage), partner(distance)),
                device_id_type=pl.DeviceIdType.MESH,
            )
            return carry

        loop(*distances(stage), greet, 0)
        met += devices - distances(stage)[0]

    pairs = (
        (filt_hbm, filt), (gate_hbm, gate), (value_hbm, value), (weight_hbm, weight),
        (outer_hbm, outer), (skip_hbm, skip), (table_hbm, table), (back_hbm, back_table),
    )
    loads = [pltpu.make_async_copy(src, dst, load_sem.at[i]) for i, (src, dst) in enumerate(pairs)]
    for load in loads:
        load.start()

    def lanes_of(share, tile):
        begin = (share * share_tiles + tile) * LANES
        return pl.ds(pl.multiple_of(begin, LANES), LANES)

    def pack(source, share, store):
        for tile in range(share_tiles):
            lanes = lanes_of(share, tile)
            parts = [source(q * piece, piece, lanes) for q in range(count)]
            for q, part in enumerate(exchange_groups(parts, width)):
                store(tile * count + q, part)

    def unpack(read, tile):
        parts = [read(tile * count + q).astype(jnp.float32) for q in range(count)]
        return exchange_groups(parts, width)

    def exchange(span, group, sent, landed, send_sem, recv_sem, act):
        def step(distance, carry):
            copy = pltpu.make_async_remote_copy(
                src_ref=sent(partner(distance)),
                dst_ref=landed,
                send_sem=send_sem.at[distance],
                recv_sem=recv_sem.at[distance],
                device_id=device_at(group, partner(distance)),
                device_id_type=pl.DeviceIdType.MESH,
            )
            act(copy)
            return carry

        loop(*span, step, 0)

    def filters(act):
        exchange(
            (1, devices), mine, lambda i: send_h.at[i], recv_h.at[me], h_send, h_recv, act
        )

    def values(stage, act):
        exchange(
            distances(stage), ahead(stage), lambda i: send_g.at[ahead(stage), i],
            recv_g.at[mine if crossed else stage, me], g_send.at[stage], g_recv.at[stage], act,
        )

    def results(stage, act):
        exchange(
            distances(stage), behind(stage), lambda i: send_r.at[behind(stage), i],
            recv_r.at[mine if crossed else stage, me], r_send.at[stage], r_recv.at[stage], act,
        )

    def start(copy):
        copy.start()

    def arrived(copy):
        copy.wait_recv()

    def left(copy):
        copy.wait_send()

    pl.semaphore_wait(barrier, met)
    rim_copies = [
        pltpu.make_async_remote_copy(
            src_ref=stream.at[rows - rim.shape[1] :],
            dst_ref=rim.at[i],
            send_sem=rim_send.at[i],
            recv_sem=rim_recv.at[i],
            device_id={"groups": mine, "ctx": partner(1)},
            device_id_type=pl.DeviceIdType.MESH,
        )
        for i, stream in enumerate((gate_hbm, outer_hbm, value_hbm))
    ]
    for i in (0, 2, 1):
        rim_copies[i].start()

    loads[0].wait()
    for held in range(filters_held):

        def store_filter(device, part):
            send_h[device, held] = part.astype(send_h.dtype)

        pack(
            lambda r, n, lanes: filt[r : r + n, lanes].astype(jnp.float32),
            mine if crossed else held, store_filter,
        )
    filters(start)

    def short(i, r, n, lanes):
        taps = weight[i, :, lanes].astype(jnp.float32)
        total = None
        for offset in range(taps.shape[0]):
            begin = r + RIM - offset
            term = taps[offset : offset + 1] * ext[i, begin : begin + n, lanes]
            total = term if total is None else total + term
        return total

    def gated(r, n, lanes):
        result = short(0, r, n, lanes) * short(2, r, n, lanes)
        kept[r : r + n, lanes] = result
        return result

    ext[:, :RIM, :] = jnp.zeros((3, RIM, channels), jnp.float32)
    for load in loads[1:4]:
        load.wait()
    ext[0, RIM:, :] = gate[...].astype(jnp.float32)
    ext[2, RIM:, :] = value[...].astype(jnp.float32)
    for stage in range(shares):

        def store_value(device, part):
            send_g[ahead(stage), device] = part

        pack(gated, ahead(stage), store_value)
    for i in (0, 2):
        rim_copies[i].wait()
        last = rim[i].astype(jnp.float32)[rim.shape[1] - RIM :]
        ext[i, :RIM, :] = jnp.where(me > 0, last, 0.0)
    first_lanes = lane_group(RIM, width) == 0
    for stage in range(shares):
        share = ahead(stage)
        for tile in range(share_tiles):
            block = gated(0, RIM, lanes_of(share, tile))
            for q in range(count):
                device = tile * count + q
                moved = pltpu.roll(block, (LANES - q * width) % LANES, 1)
                send_g[share, device, :RIM] = jnp.where(
                    first_lanes, moved, send_g[share, device, :RIM]
                )
        values(stage, start)
    for stage in range(1 if crossed else shares):
        recv_g[behind(stage), pl.ds(me, 1)] = send_g[ahead(stage), pl.ds(me, 1)]
    recv_h[pl.ds(me, 1)] = send_h[pl.ds(me, 1)]
    for load in loads[4:]:
        load.wait()

    rim_copies[1].wait()
    ext[1, :RIM, :] = jnp.where(me > 0, rim[1].astype(jnp.float32)[rim.shape[1] - RIM :], 0.0)
    ext[1, RIM:, :] = outer[...].astype(jnp.float32)
    for tile in range(tiles):
        lanes = slice(tile * LANES, (tile + 1) * LANES)
        for q in range(count):
            at = slice(q * piece, (q + 1) * piece)
            first = short(1, q * piece, piece, lanes)
            factor[at, lanes] = first
            kept[at, lanes] = skip[:, lanes] * kept[at, lanes] * first

    chunk = 32
    group = lane_group(chunk, width)
    sign = 1.0 - 2.0 * (lax.broadcasted_iota(jnp.int32, (chunk, LANES), 0) % 2).astype(jnp.float32)

    def rows_at(begin):
        if isinstance(begin, int):
            return slice(begin, begin + chunk)
        return pl.ds(pl.multiple_of(begin, chunk), chunk)

    def read(ref, begin, tile):
        lanes = slice(tile * LANES, (tile + 1) * LANES)
        return (
            ref[rows_at(begin), lanes],
            ref[rows_at(rows + begin), lanes],
        )

    def shifted(blocks, tile, places):
        turned = pltpu.roll(blocks[tile], places * width, 1)
        before = pltpu.roll(blocks[tile - 1], places * width, 1) if tile > 0 else 0.0
        return jnp.where(group >= places, turned, before)

    filters(arrived)
    taps = jnp.concatenate(
        [
            jnp.concatenate(unpack(lambda i: recv_h[i, held], tile), axis=0)
            for held in range(filters_held)
            for tile in range(share_tiles)
        ],
        axis=1,
    ).astype(jnp.bfloat16)
    spec_h[...] = dot(table[0], taps) + dot(table[1], taps)
    for held in range(filters_held):

        def spread_chunk(index, carry):
            begin = index * chunk
            at = rows_at(begin)
            loaded = [
                read(spec_h, begin, held * share_tiles + tile) for tile in range(share_tiles)
            ]
            real = [pair[0] for pair in loaded]
            imag = [pair[1] for pair in loaded]
            for tile in range(share_tiles):
                both = (
                    real[tile] - sign * shifted(imag, tile, 1),
                    imag[tile] + sign * shifted(real, tile, 1),
                )
                for part, block in enumerate(both):
                    for k, wide in enumerate(spread_groups(block, width)):
                        spread[held, k, tile, part, at, :] = wide
            return carry

        loop(0, rows // chunk, spread_chunk, 0)

    for stage in range(shares):
        share, held = behind(stage), 0 if crossed else stage
        values(stage, arrived)
        block = jnp.concatenate(
            [
                jnp.concatenate(unpack(lambda i: recv_g[share, i], tile), axis=0)
                for tile in range(share_tiles)
            ],
            axis=1,
        )
        high, low = halves(block)
        both = dot(table[0], jnp.concatenate([high, low], axis=1))
        spec[...] = both[:, :wide] + both[:, wide:] + dot(table[1], high)

        def product_chunk(index, carry):
            begin = index * chunk
            at = rows_at(begin)
            also = rows_at(rows + begin)
            loaded = [read(spec, begin, tile) for tile in range(share_tiles)]
            real = [pair[0] for pair in loaded]
            imag = [pair[1] for pair in loaded]

            def step(k, sums):
                sums = list(sums)
                moved_real = [shifted(real, tile, k) for tile in range(share_tiles)]
                moved_imag = [shifted(imag, tile, k) for tile in range(share_tiles)]
                for apart in range(share_tiles):
                    kr = spread[held, k, apart, 0, at, :]
                    ki = spread[held, k, apart, 1, at, :]
                    for tile in range(apart, share_tiles):
                        xr, xi = moved_real[tile - apart], moved_imag[tile - apart]
                        sums[2 * tile] = sums[2 * tile] + (xr * kr - xi * ki)
                        sums[2 * tile + 1] = sums[2 * tile + 1] + (xr * ki + xi * kr)
                return tuple(sums)

            zero = jnp.zeros((chunk, LANES), jnp.float32)
            sums = loop(0, count, step, (zero,) * (2 * share_tiles))
            for tile in range(share_tiles):
                lanes = slice(tile * LANES, (tile + 1) * LANES)
                for where, total in ((at, sums[2 * tile]), (also, sums[2 * tile + 1])):
                    high, low = halves(total)
                    prod[where, lanes] = high
                    prod[where, slice(wide + lanes.start, wide + lanes.stop)] = low
            return carry

        loop(0, rows // chunk, product_chunk, 0)

        both = dot(back_table[0], prod[...])
        long_rows = both[:, :wide] + both[:, wide:] + dot(back_table[1], prod[:, :wide])
        for tile in range(share_tiles):
            lanes = slice(tile * LANES, (tile + 1) * LANES)
            parts = [long_rows[q * piece : (q + 1) * piece, lanes] for q in range(count)]
            for q, part in enumerate(exchange_groups(parts, width)):
                send_r[share, tile * count + q] = part
        results(stage, start)
        if stage == 0 or not crossed:
            recv_r[share, pl.ds(me, 1)] = send_r[share, pl.ds(me, 1)]

    for stage in range(shares):
        share = ahead(stage)
        results(stage, arrived)
        for tile in range(share_tiles):
            lanes = lanes_of(share, tile)
            for q, part in enumerate(unpack(lambda i: recv_r[share, i], tile)):
                at = slice(q * piece, (q + 1) * piece)
                out[at, lanes] = (factor[at, lanes] * part + kept[at, lanes]).astype(out.dtype)
    filters(left)
    for stage in range(shares):
        values(stage, left)
        results(stage, left)


def body(gate_stream, outer_stream, value_stream, short_weight, long_filter, skip_gain):
    devices, groups = lax.axis_size("ctx"), lax.axis_size("groups")
    rows, channels = gate_stream.shape
    tiles = channels // LANES
    shares = 2
    while shares > 1 and (tiles % shares or rows * channels // (devices * shares * LANES) < 16):
        shares -= 1
    crossed = shares == groups > 1
    held = 1 if crossed else shares
    width = channels // (devices * shares)
    count = LANES // width
    piece = rows // count
    share_tiles = tiles // shares
    table = transform_table(rows)
    filter_type = jnp.bfloat16 if piece % 16 == 0 else jnp.float32
    full = pltpu.VMEM((shares, devices, piece, LANES), jnp.float32)
    part = pltpu.VMEM((devices, held, piece, LANES), filter_type)
    many = pltpu.SemaphoreType.DMA((shares, devices))
    operands = (
        gate_stream, outer_stream, value_stream, short_weight, long_filter, skip_gain[None, :],
        jnp.asarray(split(table)), jnp.asarray(split(table.T / rows)),
    )
    return pl.pallas_call(
        functools.partial(kernel, devices, groups, shares, crossed),
        out_shape=jax.ShapeDtypeStruct((rows, channels), jnp.bfloat16),
        in_specs=[pl.BlockSpec(memory_space=pltpu.HBM)] * len(operands),
        out_specs=pl.BlockSpec(memory_space=pltpu.VMEM),
        scratch_shapes=[
            *(pltpu.VMEM(each.shape, each.dtype) for each in operands),
            pltpu.VMEM((3, RIM + rows, channels), jnp.float32),
            pltpu.VMEM((3, 16, channels), jnp.bfloat16),
            part, part, full, full, full, full,
            pltpu.VMEM((2 * rows, share_tiles * LANES), jnp.float32),
            pltpu.VMEM((2 * rows, held * share_tiles * LANES), jnp.float32),
            pltpu.VMEM((held, count, share_tiles, 2, rows, LANES), jnp.float32),
            pltpu.VMEM((2 * rows, 2 * share_tiles * LANES), jnp.bfloat16),
            pltpu.VMEM((rows, channels), jnp.float32),
            pltpu.VMEM((rows, channels), jnp.float32),
            pltpu.SemaphoreType.DMA((len(operands),)),
            pltpu.SemaphoreType.DMA((3,)),
            pltpu.SemaphoreType.DMA((3,)),
            pltpu.SemaphoreType.DMA((devices,)),
            pltpu.SemaphoreType.DMA((devices,)),
            many, many, many, many,
        ],
        compiler_params=pltpu.CompilerParams(
            collective_id=0, has_side_effects=True, vmem_limit_bytes=55040 * 1024
        ),
        cost_estimate=pl.CostEstimate(
            flops=2 * 16 * rows * rows * channels, bytes_accessed=4 * rows * channels, transcendentals=0
        ),
    )(*operands)


def solution(mesh):
    placed = (
        P(("groups", "ctx"), "ch"),
        P(("groups", "ctx"), "ch"),
        P(("groups", "ctx"), "ch"),
        P(None, None, "ch"),
        P("ctx", "ch"),
        P("ch"),
    )
    return jax.shard_map(
        body, mesh=mesh, in_specs=placed, out_specs=P(("groups", "ctx"), "ch"), check_vma=False
    )
```
